512 devices in a mesh: lat: 16 (over z), lon: 16 (over x, y_lo, core), dp: 2 (over y_hi).
Axes of the slice: x: 4, y: 4 (y_hi: 2, y_lo: 2; y = y_hi * 2 + y_lo), z: 16, core: 2. Of those that a mesh axis runs over, the one named last changes fastest.
Arguments:
- input_field: bfloat16 [2, 64, 1024, 256], P('dp', 'lat', 'lon'), may hold values from -6 to 6
- cotangent: bfloat16 [2, 64, 1024, 256], P('dp', 'lat', 'lon'), may hold values from -6 to 6
- channel_weight: bfloat16 [9, 256, 256], replicated, may hold values from -0.125 to 0.125
- basis_filter: bfloat16 [9, 64, 3, 17], replicated, may hold values from -0.875 to 0.875
- reach_cols: int32 [64], replicated, may hold values from 1 to 8, as said below
Outputs:
- output_field: bfloat16 [2, 64, 1024, 256], P('dp', 'lat', 'lon')
- grad_input: bfloat16 [2, 64, 1024, 256], P('dp', 'lat', 'lon')
- grad_weight: bfloat16 [9, 256, 256], P(None, None, 'lon')
The draws below stay inside these ranges and needn't reach their ends.
Inputs may be any that keep to these rules, and one draw needn't show every extreme that they name: reach_cols is 8 at the first and the last row of the grid.
All inputs are finite; a program needn't handle non-finite values.
Results may differ from the reference program's by a relative error of at most 0.005.
Values may be sent and summed in bfloat16 or wider, within the bound.
A program may use at most 128 MiB of HBM per device.

```python
import math
import jax
import jax.numpy as jnp
from jax import lax

CHANNELS = 256
BASIS = 9
LAT_REACH = 1
LON_REACH = 8
NLAT = 64
NLON = 1024
BATCH = 2


def draw_reach_cols(key, part):
    key = jax.random.fold_in(key, 11)
    row_ids = jnp.arange(NLAT, dtype=jnp.int32)
    polar = jnp.minimum(row_ids, NLAT - 1 - row_ids)
    extra = jax.random.randint(key, (NLAT,), 0, 2, dtype=jnp.int32)
    return jnp.minimum(LON_REACH, 1 + extra + 2 * LON_REACH // (polar + 2)).astype(jnp.int32)


def raised(entries, key, source, target, parts, factor):
    def block_of(axis_at):
        return (jnp.arange(entries.shape[axis_at]) // (entries.shape[axis_at] // parts)).reshape((-1,) + (1,) * (entries.ndim - 1 - axis_at))

    first = jax.random.permutation(key, parts)[block_of(target)]
    far = (block_of(target) + parts // 2) % parts
    return jnp.where((block_of(source) == first) | (block_of(source) == far), factor * entries, entries)


def block_scale(stream_key, extent, split, smallest, largest):
    def one(position, shards_of):
        draws = jax.random.uniform(jax.random.fold_in(jax.random.fold_in(stream_key, 6), position), (shards_of,), jnp.float32, smallest / len(split), largest / len(split))
        return jnp.repeat(jnp.exp(draws), extent[position] // shards_of).reshape((-1,) + (1,) * (len(extent) - position - 1))

    loudness = one(*split[0])
    for cut in split[1:]:
        loudness = loudness * one(*cut)
    return loudness


def noise(key, extent, deviation, most, split=(), kind=jnp.bfloat16):
    loudness = block_scale(key, extent, split, -0.22, 0.18) if split else 1.0
    entries = jax.random.normal(key, extent, jnp.float32) * deviation * loudness
    return jnp.minimum(jnp.maximum(entries, -most), most).astype(kind)


def noise_with(rng, dims, width, most, pieces, heavy, kind=jnp.bfloat16):
    array = width * jax.random.normal(rng, dims, jnp.float32)
    if pieces:
        array = array * block_scale(rng, dims, pieces, -0.22, 0.18)
    return jnp.clip(raised(array, jax.random.fold_in(rng, 3), *heavy), -most, most).astype(kind)


def setup_inputs(seed: int = 0) -> dict:
    arg_keys = jax.random.split(jax.random.key(seed), 6)
    input_field = noise(arg_keys[0], (BATCH, NLAT, NLON, CHANNELS), 1.0, 6.0, ((0, 2), (1, 16), (2, 16)))
    cotangent = noise_with(arg_keys[1], (BATCH, NLAT, NLON, CHANNELS), 1.0, 6.0, ((0, 2), (1, 16), (2, 16)), (2, 3, 16, 2.0))
    channel_weight = noise(arg_keys[2], (BASIS, CHANNELS, CHANNELS), (BASIS * CHANNELS) ** -0.5, 0.125)
    basis_filter = noise(arg_keys[3], (BASIS, NLAT, 2 * LAT_REACH + 1, 2 * LON_REACH + 1), ((2 * LAT_REACH + 1) * (2 * LON_REACH + 1)) ** -0.5, 0.875)
    reach_cols = draw_reach_cols(jax.random.fold_in(arg_keys[5], 71), 0)
    return dict(input_field=input_field, cotangent=cotangent, channel_weight=channel_weight, basis_filter=basis_filter, reach_cols=reach_cols)


def masked_filter(basis_filter, reach_cols):
    offsets = jnp.abs(jnp.arange(2 * LON_REACH + 1, dtype=jnp.int32) - LON_REACH)
    inside = (offsets[None, :] <= reach_cols[:, None]).astype(jnp.float32)
    return basis_filter.astype(jnp.float32) * inside[None, :, None, :]

def reference(input_field, cotangent, channel_weight, basis_filter, reach_cols):
    coeff_full = masked_filter(basis_filter, reach_cols)
    weight_wide = channel_weight.astype(jnp.float32)
    span_count = 2 * LAT_REACH + 1
    tap_count = 2 * LON_REACH + 1
    padded_field = jnp.pad(input_field.astype(jnp.float32), ((0, 0), (LAT_REACH, LAT_REACH), (0, 0), (0, 0)))
    highest = lax.Precision.HIGHEST

    def one_row(carried, row_index):
        accumulated, weight_sum = carried
        window_rows = lax.dynamic_slice_in_dim(padded_field, row_index, span_count, 1)
        window = jnp.stack([jnp.roll(window_rows, LON_REACH - column_tap, axis=2) for column_tap in range(tap_count)], axis=2)
        row_coeff = lax.dynamic_index_in_dim(coeff_full, row_index, 1, keepdims=False)
        conv_row = jnp.einsum('kae,baenc->kbnc', row_coeff, window, precision=highest)
        conv_wide = lax.optimization_barrier(conv_row.astype(jnp.bfloat16)).astype(jnp.float32)
        output_row = jnp.einsum('kbnc,kcd->bnd', conv_wide, weight_wide, precision=highest).astype(jnp.bfloat16)
        cot_row = lax.dynamic_index_in_dim(cotangent, row_index, 1, keepdims=False).astype(jnp.float32)
        weight_sum = weight_sum + jnp.einsum('kbnc,bnd->kcd', conv_wide, cot_row, precision=highest)
        products = jnp.einsum('bnd,kcd->kbnc', cot_row, weight_wide, precision=highest)
        products = lax.optimization_barrier(products.astype(jnp.bfloat16)).astype(jnp.float32)
        for span_index in range(span_count):
            tap_sums = jnp.einsum('ke,kbnc->ebnc', row_coeff[:, span_index], products, precision=highest)
            contribution = tap_sums[0] * 0.0
            for column_tap in range(tap_count):
                contribution = contribution + jnp.roll(tap_sums[column_tap], column_tap - LON_REACH, axis=1)
            target = row_index + span_index
            current = lax.dynamic_index_in_dim(accumulated, target, 1, keepdims=False)
            accumulated = lax.dynamic_update_index_in_dim(accumulated, current + contribution, target, 1)
        return ((accumulated, weight_sum), output_row)
    start_acc = jnp.zeros((BATCH, NLAT + 2 * LAT_REACH, NLON, CHANNELS), jnp.float32)
    start_sum = jnp.zeros((BASIS, CHANNELS, CHANNELS), jnp.float32)
    (accumulated, weight_sum), output_rows = lax.scan(one_row, (start_acc, start_sum), jnp.arange(NLAT, dtype=jnp.int32))
    output_field = jnp.moveaxis(output_rows, 0, 1)
    grad_input = accumulated[:, LAT_REACH:LAT_REACH + NLAT].astype(jnp.bfloat16)
    grad_weight = (weight_sum * (1.0 / math.sqrt(BATCH * NLAT * NLON))).astype(jnp.bfloat16)
    return (output_field, grad_input, grad_weight)
```

```python
import functools
import math

import jax
import jax.numpy as jnp
from jax import lax
from jax.experimental import pallas as pl
from jax.experimental.pallas import tpu as pltpu
from jax.sharding import PartitionSpec as P

MESH = pl.DeviceIdType.MESH
F32 = jnp.float32
BF16 = jnp.bfloat16


def kernel_body(sizes, coeff_ref, field_hbm, cot_hbm, weight_hbm, out_hbm, gin_hbm, gw_hbm,
                win, edge, weight, fband, bband, conv, cot_t, a_send, a_recv, b_send, b_recv,
                c_send, final, out_v, gin_v, local_sem, halo_send, halo_recv,
                a_ssem, a_rsem, b_ssem, b_rsem, c_ssem, c_rsem):
    nz, nlon, ndp, basis, rows, cols, chans, taps = sizes
    reach = taps // 2
    nq = nlon // 2
    blk = chans // nlon
    scale = 1.0 / math.sqrt(ndp * nz * rows * nlon * cols)
    z = lax.axis_index("lat")
    lon = lax.axis_index("lon")
    dp = lax.axis_index("dp")
    q = lon // 2
    core = lon % 2
    mate = q * 2 + 1 - core
    block = cols + 2 * reach
    side = 2 * reach
    halves = 2
    half = chans // halves

    loads = []
    for n, src in enumerate((field_hbm, cot_hbm)):
        loads.append(pltpu.make_async_copy(
            src.at[0], win.at[n, core, pl.ds(1, rows), pl.ds(side, cols)], local_sem.at[n]))
    loads.append(pltpu.make_async_copy(weight_hbm, weight, local_sem.at[2]))
    for load in loads:
        load.start()

    barrier = pltpu.get_barrier_semaphore()
    signals = 0

    def greet(zz, ll, dd):
        pl.semaphore_signal(barrier, inc=1, device_id={"lat": zz, "lon": ll, "dp": dd},
                            device_id_type=MESH)

    up = lax.rem(z + 1, nz)
    down = lax.rem(z + nz - 1, nz)
    q_next = lax.rem(q + 1, nq)
    q_prev = lax.rem(q + nq - 1, nq)
    greet(z, mate, dp)
    signals += 1
    for zz in (down, up):
        for cc in range(2):
            greet(zz, q * 2 + cc, dp)
            signals += 1
    for zz in (down, z, up):
        greet(zz, q_prev * 2 + 1, dp)
        greet(zz, q_next * 2, dp)
        signals += 2
    for r in range(1, nq):
        greet(z, lax.rem(q + r, nq) * 2 + core, dp)
        signals += 1
    for r in range(1, nz * ndp):
        place = lax.rem(dp * nz + z + r, nz * ndp)
        greet(lax.rem(place, nz), lon, place // nz)
        signals += 1

    lanes = 3 * block + side
    tap_lane = lax.broadcasted_iota(jnp.int32, (128, lanes), 0)
    out_lane = lax.broadcasted_iota(jnp.int32, (128, lanes), 1)

    def make_band(dst, transposed):
        rowvec = jnp.zeros((rows * 16, lanes), F32)
        for a in range(3):
            if transposed:
                picked = coeff_ref[2 - a, pl.ds(16 * a, rows * 16), :]
                hit = (out_lane == reach + block * a + (taps - 1) - tap_lane) & (tap_lane < taps)
            else:
                picked = coeff_ref[a, pl.ds(16, rows * 16), :]
                hit = (out_lane == reach + block * a + tap_lane) & (tap_lane < taps)
            rowvec = rowvec + jnp.dot(picked, jnp.where(hit, 1.0, 0.0).astype(BF16),
                                      preferred_element_type=F32)
        for i in range(rows):
            for k in range(basis):
                row = jnp.broadcast_to(rowvec[i * 16 + k:i * 16 + k + 1, :], (cols, lanes))
                dst[i, pl.ds(k * cols, cols), :] = pltpu.roll(
                    row, 0, 1, stride=1, stride_axis=0).astype(BF16)

    make_band(fband, False)

    pl.semaphore_wait(barrier, signals)

    far = lax.rem(q + nq - 1 + 2 * core, nq)
    started = []

    def send(src, dst, slot, zz, ll):
        copy = pltpu.make_async_remote_copy(
            src_ref=src, dst_ref=dst, send_sem=halo_send.at[slot[0]], recv_sem=halo_recv.at[slot[1]],
            device_id={"lat": zz, "lon": ll, "dp": dp}, device_id_type=MESH)
        copy.start()
        started.append(copy)

    for n, src in enumerate((field_hbm, cot_hbm)):
        base = n * 11
        for zz, row, place, which in ((up, rows - 1, 0, 0), (down, 0, rows + 1, 1)):
            for cc in range(2):
                send(src.at[0, row], win.at[n, core, place, pl.ds(side, cols)],
                     (base + which * 2 + cc, base + which * 2 + core), zz, q * 2 + cc)
        edge_cols = pl.ds(pl.multiple_of(core * (cols - side), 16), side)
        for cc in range(2):
            send(src.at[0, :, edge_cols], edge.at[n, 1 - core, pl.ds(1, rows)],
                 (base + 4 + cc, base + 4 + 1 - core), z, far * 2 + cc)
        for zz, row, place, which in ((up, rows - 1, 0, 0), (down, 0, rows + 1, 1)):
            for cc in range(2):
                send(src.at[0, row, edge_cols], edge.at[n, 1 - core, place],
                     (base + 6 + which * 2 + cc, base + 6 + which * 2 + 1 - core), zz, far * 2 + cc)
        send(src.at[0], win.at[n, core, pl.ds(1, rows), pl.ds(side, cols)],
             (base + 10, base + 10), z, mate)

    make_band(bband, True)

    for load in loads:
        load.wait()
    for n in range(2):
        base = n * 11
        row_like = win.at[n, 0, 0, pl.ds(side, cols)]
        for s in range(4):
            pltpu.make_async_copy(row_like, row_like, halo_recv.at[base + s]).wait()
        edge_like = edge.at[n, 0, pl.ds(1, rows)]
        for s in range(4, 6):
            pltpu.make_async_copy(edge_like, edge_like, halo_recv.at[base + s]).wait()
        corner_like = edge.at[n, 0, 0]
        for s in range(6, 10):
            pltpu.make_async_copy(corner_like, corner_like, halo_recv.at[base + s]).wait()
        all_like = win.at[n, 0, pl.ds(1, rows), pl.ds(side, cols)]
        pltpu.make_async_copy(all_like, all_like, halo_recv.at[base + 10]).wait()

    def blank(place):
        for n in range(2):
            for s in range(2):
                win[n, s, place, pl.ds(side, cols), :] = jnp.zeros((cols, chans), BF16)
                edge[n, s, place] = jnp.zeros((side, chans), BF16)

    @pl.when(z == 0)
    def _():
        blank(0)

    @pl.when(z == nz - 1)
    def _():
        blank(rows + 1)

    first_half = lax.broadcasted_iota(jnp.int32, (side, chans), 0) < reach
    nothing = jnp.zeros((side, chans), F32)
    for n in range(2):
        for s in range(2):
            for r in range(rows + 3):
                if r == 0:
                    before = nothing
                elif s == 0:
                    before = win[n, 1, r - 1, pl.ds(side, side), :].astype(F32)
                else:
                    before = edge[n, 1, r - 1].astype(F32)
                if r == rows + 2:
                    after = nothing
                elif s == 0:
                    after = edge[n, 0, r].astype(F32)
                else:
                    after = win[n, 0, r, pl.ds(cols, side), :].astype(F32)
                win[n, s, r, pl.ds(0, side), :] = jnp.where(first_half, before, after).astype(BF16)

    def window(n, s, i):
        return jnp.concatenate(
            [win[n, s, i], win[n, s, i + 1], win[n, s, i + 2], win[n, s, i + 3, pl.ds(0, side), :]],
            axis=0)

    for s in range(2):
        for i in range(rows):
            part = jnp.dot(fband[i], window(0, s, i), preferred_element_type=F32)
            conv[:, s * rows + i] = part.astype(BF16).reshape(basis, cols, chans)

    for s in range(2):
        for i in range(rows):
            row = win[1, s, i + 1, pl.ds(side, cols), :].astype(F32)
            if i % 2 == 0:
                held = row
            else:
                pair = jnp.concatenate([held, row], axis=0)
                cot_t[:, :, :, pl.ds((s * rows + i - 1) * cols, 2 * cols)] = pair.T.astype(
                    BF16).reshape(nq, 2, blk, 2 * cols)

    mine_t = cot_t[:, core].reshape(nq * blk, 2 * rows * cols)
    for k in range(basis):
        terms = jnp.dot(mine_t, conv[k].reshape(2 * rows * cols, chans), preferred_element_type=F32)
        a_send[:, k] = terms.astype(BF16).reshape(nq, blk, chans)

    a_copies = []
    for r in range(1, nq):
        to = lax.rem(q + r, nq)
        copy = pltpu.make_async_remote_copy(
            src_ref=a_send.at[to], dst_ref=a_recv.at[r - 1], send_sem=a_ssem.at[r - 1],
            recv_sem=a_rsem.at[r - 1],
            device_id={"lat": z, "lon": to * 2 + core, "dp": dp}, device_id_type=MESH)
        copy.start()
        a_copies.append(copy)

    total = jnp.zeros((rows * cols, chans), F32)
    for k in range(basis):
        own = conv[k, pl.ds(core * rows, rows)].reshape(rows * cols, chans)
        total = total + jnp.dot(own, weight[k], preferred_element_type=F32)
    out_v[...] = total.astype(BF16).reshape(rows, cols, chans)
    out_copy = pltpu.make_async_copy(out_v, out_hbm.at[0], local_sem.at[0])
    out_copy.start()

    for i in range(rows):
        wide = jnp.concatenate(
            [win[1, core, i], win[1, core, i + 1], win[1, core, i + 2],
             win[1, core, i + 3, pl.ds(0, side), :]], axis=0)
        part = jnp.dot(bband[i], wide, preferred_element_type=F32)
        conv[:, i] = part.astype(BF16).reshape(basis, cols, chans)
    total = jnp.zeros((rows * cols, chans), F32)
    for k in range(basis):
        own = conv[k, pl.ds(0, rows)].reshape(rows * cols, chans)
        total = total + lax.dot_general(own, weight[k], (((1,), (1,)), ((), ())),
                                        preferred_element_type=F32)
    gin_v[...] = total.astype(BF16).reshape(rows, cols, chans)
    gin_copy = pltpu.make_async_copy(gin_v, gin_hbm.at[0], local_sem.at[1])
    gin_copy.start()

    for copy in a_copies:
        copy.wait_recv()
    for k in range(basis):
        summed = a_send[q, k].astype(F32)
        for r in range(nq - 1):
            summed = summed + a_recv[r, k].astype(F32)
        b_send[k] = summed.astype(BF16)

    def keeper(k):
        return (nz * k) // basis

    def tile(ref, k, h):
        return ref.at[k, :, pl.ds(h * half, half)]

    me = dp * nz + z
    for k in range(basis):
        for h in range(halves):
            away = jnp.logical_or(z != keeper(k), dp != h)

            @pl.when(away)
            def _(k=k, h=h):
                pltpu.make_async_remote_copy(
                    src_ref=tile(b_send, k, h), dst_ref=b_recv.at[me],
                    send_sem=b_ssem.at[k * halves + h], recv_sem=b_rsem.at[me],
                    device_id={"lat": keeper(k), "lon": lon, "dp": h}, device_id_type=MESH).start()

    my_k = (basis * z + nz - 1) // nz
    keeps = jnp.logical_and(my_k < basis, (nz * my_k) // basis == z)
    my_k = jnp.minimum(my_k, basis - 1)
    my_lanes = pl.ds(pl.multiple_of(dp * half, half), half)

    @pl.when(keeps)
    def _():
        for r in range(1, nz * ndp):
            place = lax.rem(me + r, nz * ndp)
            pltpu.make_async_copy(b_recv.at[place], b_recv.at[place], b_rsem.at[place]).wait()
        b_recv[me] = b_send[my_k, :, my_lanes]
        summed = jnp.zeros((blk, half), F32)
        for r in range(nz * ndp):
            summed = summed + b_recv[r].astype(F32)
        c_send[...] = (summed * scale).astype(BF16)
        for r in range(1, nz * ndp):
            place = lax.rem(me + r, nz * ndp)
            pltpu.make_async_remote_copy(
                src_ref=c_send, dst_ref=final.at[my_k, :, my_lanes],
                send_sem=c_ssem.at[r], recv_sem=c_rsem.at[my_k * halves + dp],
                device_id={"lat": lax.rem(place, nz), "lon": lon, "dp": place // nz},
                device_id_type=MESH).start()
        final[my_k, :, my_lanes] = c_send[...]

    for k in range(basis):
        for h in range(halves):
            away = jnp.logical_or(z != keeper(k), dp != h)

            @pl.when(away)
            def _(k=k, h=h):
                spot = tile(final, k, h)
                pltpu.make_async_copy(spot, spot, c_rsem.at[k * halves + h]).wait()

    gw_copy = pltpu.make_async_copy(final, gw_hbm, local_sem.at[2])
    gw_copy.start()

    for copy in started:
        copy.wait_send()
    for copy in a_copies:
        copy.wait_send()
    for k in range(basis):
        for h in range(halves):
            away = jnp.logical_or(z != keeper(k), dp != h)

            @pl.when(away)
            def _(k=k, h=h):
                spot = tile(b_send, k, h)
                pltpu.make_async_copy(spot, spot, b_ssem.at[k * halves + h]).wait()

    @pl.when(keeps)
    def _():
        for r in range(1, nz * ndp):
            pltpu.make_async_copy(c_send, c_send, c_ssem.at[r]).wait()

    out_copy.wait()
    gin_copy.wait()
    gw_copy.wait()


def on_device(input_field, cotangent, channel_weight, basis_filter, reach_cols):
    _, rows, cols, chans = input_field.shape
    basis, nlat, spans, taps = basis_filter.shape
    reach = taps // 2
    nz, nlon, ndp = (lax.axis_size(name) for name in ("lat", "lon", "dp"))
    nq = nlon // 2
    blk = chans // nlon
    block = cols + 2 * reach
    side = 2 * reach
    lanes = spans * block + side

    first = lax.axis_index("lat") * rows
    offsets = jnp.abs(jnp.arange(taps, dtype=jnp.int32) - reach)
    near = lax.dynamic_slice_in_dim(jnp.pad(basis_filter, ((0, 0), (1, 1), (0, 0), (0, 0))),
                                    first, rows + 2, 1)
    near_reach = lax.dynamic_slice_in_dim(jnp.pad(reach_cols, (1, 1)), first, rows + 2, 0)
    inside = offsets[None, :] <= near_reach[:, None]
    near = jnp.where(inside[None, :, None, :], near, 0)
    coeff = jnp.transpose(near, (2, 1, 0, 3))
    coeff = jnp.pad(coeff, ((0, 0), (0, 0), (0, 16 - basis), (0, 128 - taps)))
    coeff = coeff.reshape(spans, (rows + 2) * 16, 128).astype(BF16)

    sizes = (nz, nlon, ndp, basis, rows, cols, chans, taps)
    vmem = pl.BlockSpec(memory_space=pltpu.VMEM)
    anywhere = pl.BlockSpec(memory_space=pl.ANY)
    dma = pltpu.SemaphoreType.DMA
    group = nz * ndp
    out, gin, gw = pl.pallas_call(
        functools.partial(kernel_body, sizes),
        out_shape=(jax.ShapeDtypeStruct(input_field.shape, BF16),
                   jax.ShapeDtypeStruct(input_field.shape, BF16),
                   jax.ShapeDtypeStruct((basis, blk, chans), BF16)),
        in_specs=[vmem, anywhere, anywhere, anywhere],
        out_specs=(anywhere, anywhere, anywhere),
        scratch_shapes=[
            pltpu.VMEM((2, 2, rows + 3, block, chans), BF16),
            pltpu.VMEM((2, 2, rows + 2, side, chans), BF16),
            pltpu.VMEM((basis, chans, chans), BF16),
            pltpu.VMEM((rows, basis * cols, lanes), BF16),
            pltpu.VMEM((rows, basis * cols, lanes), BF16),
            pltpu.VMEM((basis, 2 * rows, cols, chans), BF16),
            pltpu.VMEM((nq, 2, blk, 2 * rows * cols), BF16),
            pltpu.VMEM((nq, basis, blk, chans), BF16),
            pltpu.VMEM((max(nq - 1, 1), basis, blk, chans), BF16),
            pltpu.VMEM((basis, blk, chans), BF16),
            pltpu.VMEM((group, blk, chans // 2), BF16),
            pltpu.VMEM((blk, chans // 2), BF16),
            pltpu.VMEM((basis, blk, chans), BF16),
            pltpu.VMEM((rows, cols, chans), BF16),
            pltpu.VMEM((rows, cols, chans), BF16),
            dma((3,)), dma((22,)), dma((22,)),
            dma((max(nq - 1, 1),)), dma((max(nq - 1, 1),)),
            dma((basis * 2,)), dma((group,)), dma((group,)), dma((basis * 2,)),
        ],
        compiler_params=pltpu.CompilerParams(
            collective_id=0, has_side_effects=True, vmem_limit_bytes=48 * 1024 * 1024),
        name="disco_block",
    )(coeff, input_field, cotangent, channel_weight)
    return out, gin, jnp.transpose(gw, (0, 2, 1))


def solution(mesh):
    placed = (P("dp", "lat", "lon", None), P("dp", "lat", "lon", None), P(), P(), P())
    return jax.shard_map(
        on_device,
        mesh=mesh,
        in_specs=placed,
        out_specs=(P("dp", "lat", "lon", None), P("dp", "lat", "lon", None), P(None, None, "lon")),
        check_vma=False,
    )
```

```python
import functools
import math

import jax
import jax.numpy as jnp
from jax import lax
from jax.experimental import pallas as pl
from jax.experimental.pallas import tpu as pltpu
from jax.sharding import PartitionSpec as P

MESH = pl.DeviceIdType.MESH
F32 = jnp.float32
BF16 = jnp.bfloat16


FIRST_KEEPER = 10


def kernel_body(sizes, coeff_ref, field_hbm, cot_hbm, weight_hbm, out_v, gin_v, final,
                win, edge, cwin, cedge, cot, weight, fband, bband, conv, cot_t, a_send, a_recv,
                b_send, b_recv, c_send, local_sem, halo_send, halo_recv, a_ssem, a_rsem, b_ssem,
                b_rsem, c_ssem, c_rsem, near_sem, dp_sem):
    nz, nlon, ndp, basis, rows, cols, chans, taps = sizes
    reach = taps // 2
    nq = nlon // 2
    blk = chans // nlon
    scale = 1.0 / math.sqrt(ndp * nz * rows * nlon * cols)
    z = lax.axis_index("lat")
    lon = lax.axis_index("lon")
    dp = lax.axis_index("dp")
    q = lon // 2
    core = lon % 2
    mate = q * 2 + 1 - core
    block = cols + 2 * reach
    side = 2 * reach
    half = chans // ndp
    plane = nq * ndp

    def device(zz, ll, dd):
        return {"lat": zz, "lon": ll, "dp": dd}

    barrier = pltpu.get_barrier_semaphore()
    greeted = []

    def greet(*place):
        pl.semaphore_signal(barrier, inc=1, device_id=device(*place), device_id_type=MESH)
        greeted.append(place)

    up = lax.rem(z + 1, nz)
    down = lax.rem(z + nz - 1, nz)
    q_next = lax.rem(q + 1, nq)
    q_prev = lax.rem(q + nq - 1, nq)
    g = dp * nq + q
    for zz in (down, up):
        for cc in range(2):
            greet(zz, q * 2 + cc, dp)
    for zz in (down, up, z):
        greet(zz, q_prev * 2 + 1, dp)
        greet(zz, q_next * 2, dp)
    greet(z, mate, dp)
    for r in range(1, plane):
        place = lax.rem(g + r, plane)
        greet(z, lax.rem(place, nq) * 2 + core, place // nq)

    inside = (pl.ds(1, rows), pl.ds(side, cols))
    loads = [
        pltpu.make_async_copy(field_hbm.at[0], win.at[core, inside[0], inside[1]], local_sem.at[0]),
        pltpu.make_async_copy(cot_hbm.at[0], cot.at[core], local_sem.at[1]),
        pltpu.make_async_copy(cot_hbm.at[0], cwin.at[inside[0], inside[1]], local_sem.at[2]),
        pltpu.make_async_copy(weight_hbm, weight, local_sem.at[3]),
    ]
    for load in loads:
        load.start()

    pl.semaphore_wait(barrier, len(greeted))

    far = lax.rem(q + nq - 1 + 2 * core, nq)
    edge_cols = pl.ds(pl.multiple_of(core * (cols - side), 16), side)
    near_cols = pl.ds(pl.multiple_of((1 - core) * (cols - side), 16), side)
    started = []

    def send(src, dst, slots, zz, ll):
        copy = pltpu.make_async_remote_copy(
            src_ref=src, dst_ref=dst, send_sem=halo_send.at[slots[0]],
            recv_sem=halo_recv.at[slots[1]], device_id=device(zz, ll, dp), device_id_type=MESH)
        copy.start()
        started.append(copy)

    lat_sides = ((up, rows - 1, 0, 0), (down, 0, rows + 1, 1))
    for zz, row, place, which in lat_sides:
        for cc in range(2):
            send(field_hbm.at[0, row], win.at[core, place, inside[1]],
                 (which * 2 + cc, which * 2 + core), zz, q * 2 + cc)
    for zz, row, place, which in lat_sides:
        for cc in range(2):
            send(field_hbm.at[0, row, edge_cols], edge.at[1 - core, place],
                 (6 + which * 2 + cc, 6 + which * 2 + 1 - core), zz, far * 2 + cc)
    for cc in range(2):
        send(field_hbm.at[0, :, edge_cols], edge.at[1 - core, inside[0]],
             (4 + cc, 4 + 1 - core), z, far * 2 + cc)
    send(field_hbm.at[0], win.at[core, inside[0], inside[1]], (10, 10), z, mate)
    send(cot_hbm.at[0], cot.at[core], (11, 11), z, mate)
    for zz, row, place, which in lat_sides:
        send(cot_hbm.at[0, row], cwin.at[place, inside[1]], (12 + which, 12 + which), zz, lon)
        send(cot_hbm.at[0, row, near_cols], cedge.at[core, place], (14 + which, 14 + which),
             zz, mate)
        send(cot_hbm.at[0, row, edge_cols], cedge.at[1 - core, place], (16 + which, 16 + which),
             zz, far * 2 + 1 - core)
    send(cot_hbm.at[0, :, edge_cols], cedge.at[1 - core, inside[0]], (18, 18),
         z, far * 2 + 1 - core)

    def arrived(slot, like):
        pltpu.make_async_copy(like, like, halo_recv.at[slot]).wait()

    spans = []
    while 2 ** (len(spans) + 1) <= nz // 2:
        spans.append(2 ** len(spans))

    def tell(n):
        for way, step in ((0, spans[n]), (1, nz - spans[n])):
            pl.semaphore_signal(near_sem.at[n, way], inc=1,
                                device_id=device(lax.rem(z + step, nz), lon, dp),
                                device_id_type=MESH)

    def told(n):
        for way in range(2):
            pl.semaphore_wait(near_sem.at[n, way], 1)

    def relay(n):
        if 0 < n <= len(spans):
            told(n - 1)
        if n < len(spans):
            tell(n)

    relay(0)

    lanes = 3 * block + side
    tap_lane = lax.broadcasted_iota(jnp.int32, (128, lanes), 0)
    out_lane = lax.broadcasted_iota(jnp.int32, (128, lanes), 1)

    def make_band(dst, transposed):
        rowvec = jnp.zeros((rows * 16, lanes), F32)
        for a in range(3):
            if transposed:
                picked = coeff_ref[2 - a, pl.ds(16 * a, rows * 16), :]
                hit = (out_lane == reach + block * a + (taps - 1) - tap_lane) & (tap_lane < taps)
            else:
                picked = coeff_ref[a, pl.ds(16, rows * 16), :]
                hit = (out_lane == reach + block * a + tap_lane) & (tap_lane < taps)
            rowvec = rowvec + jnp.dot(picked, jnp.where(hit, 1.0, 0.0).astype(BF16),
                                      preferred_element_type=F32)
        for i in range(rows):
            for k in range(basis):
                row = jnp.broadcast_to(rowvec[i * 16 + k:i * 16 + k + 1, :], (cols, lanes))
                dst[i, pl.ds(k * cols, cols), :] = pltpu.roll(
                    row, 0, 1, stride=1, stride_axis=0).astype(BF16)

    make_band(fband, False)
    relay(1)

    for load in loads:
        load.wait()
    arrived(11, cot.at[0])
    for s in range(2):
        for i in range(0, rows, 2):
            pair = cot[s, pl.ds(i, 2)].reshape(2 * cols, chans).astype(F32)
            cot_t[:, :, :, pl.ds((s * rows + i) * cols, 2 * cols)] = pair.T.astype(
                BF16).reshape(nq, 2, blk, 2 * cols)

    for slot in range(4):
        arrived(slot, win.at[0, 0, inside[1]])
    for slot in range(4, 6):
        arrived(slot, edge.at[0, inside[0]])
    for slot in range(6, 10):
        arrived(slot, edge.at[0, 0])
    arrived(10, win.at[0, inside[0], inside[1]])

    def blank_field(place):
        for s in range(2):
            win[s, place, inside[1], :] = jnp.zeros((cols, chans), BF16)
            edge[s, place] = jnp.zeros((side, chans), BF16)

    @pl.when(z == 0)
    def _():
        blank_field(0)

    @pl.when(z == nz - 1)
    def _():
        blank_field(rows + 1)

    first_half = lax.broadcasted_iota(jnp.int32, (side, chans), 0) < reach
    nothing = jnp.zeros((side, chans), F32)

    def joint(before, after):
        before = nothing if before is None else before.astype(F32)
        after = nothing if after is None else after.astype(F32)
        return jnp.where(first_half, before, after).astype(BF16)

    for r in range(rows + 3):
        first, last = r == 0, r == rows + 2
        win[0, r, pl.ds(0, side), :] = joint(
            None if first else win[1, r - 1, pl.ds(side, side), :],
            None if last else edge[0, r])
        win[1, r, pl.ds(0, side), :] = joint(
            None if first else edge[1, r - 1],
            None if last else win[0, r, pl.ds(cols, side), :])

    for s in range(2):
        for i in range(rows):
            wide = jnp.concatenate([win[s, i], win[s, i + 1], win[s, i + 2],
                                    win[s, i + 3, pl.ds(0, side), :]], axis=0)
            part = jnp.dot(fband[i], wide, preferred_element_type=F32)
            conv[:, s * rows + i] = part.astype(BF16).reshape(basis, cols, chans)
    relay(2)

    mine_t = cot_t[:, core].reshape(nq * blk, 2 * rows * cols)
    for k in range(basis):
        terms = jnp.dot(mine_t, conv[k].reshape(2 * rows * cols, chans), preferred_element_type=F32)
        terms = terms.astype(BF16).reshape(nq, blk, chans)
        for h in range(ndp):
            a_send[h, :, k] = terms[:, :, h * half:(h + 1) * half]

    a_copies = []
    for r in range(1, plane):
        place = lax.rem(g + r, plane)
        to_q = lax.rem(place, nq)
        copy = pltpu.make_async_remote_copy(
            src_ref=a_send.at[place // nq, to_q], dst_ref=a_recv.at[r - 1],
            send_sem=a_ssem.at[r - 1], recv_sem=a_rsem.at[r - 1],
            device_id=device(z, to_q * 2 + core, place // nq), device_id_type=MESH)
        copy.start()
        a_copies.append(copy)

    make_band(bband, True)
    total = jnp.zeros((rows * cols, chans), F32)
    for k in range(basis):
        own = conv[k, pl.ds(core * rows, rows)].reshape(rows * cols, chans)
        total = total + jnp.dot(own, weight[k], preferred_element_type=F32)
    out_v[0] = total.astype(BF16).reshape(rows, cols, chans)

    for slot in range(12, 14):
        arrived(slot, cwin.at[0, inside[1]])
    for slot in range(14, 18):
        arrived(slot, cedge.at[0, 0])
    arrived(18, cedge.at[0, inside[0]])
    cedge[1 - core, inside[0]] = cot[1 - core, :, edge_cols, :]

    def blank_cot(place):
        cwin[place, inside[1], :] = jnp.zeros((cols, chans), BF16)
        for s in range(2):
            cedge[s, place] = jnp.zeros((side, chans), BF16)

    @pl.when(z == 0)
    def _():
        blank_cot(0)

    @pl.when(z == nz - 1)
    def _():
        blank_cot(rows + 1)

    for r in range(rows + 3):
        cwin[r, pl.ds(0, side), :] = joint(
            None if r == 0 else cedge[1, r - 1], None if r == rows + 2 else cedge[0, r])
    for i in range(rows):
        wide = jnp.concatenate(
            [cwin[i], cwin[i + 1], cwin[i + 2], cwin[i + 3, pl.ds(0, side), :]], axis=0)
        part = jnp.dot(bband[i], wide, preferred_element_type=F32)
        conv[:, i] = part.astype(BF16).reshape(basis, cols, chans)
    total = jnp.zeros((rows * cols, chans), F32)
    for k in range(basis):
        own = conv[k, pl.ds(0, rows)].reshape(rows * cols, chans)
        total = total + lax.dot_general(own, weight[k], (((1,), (1,)), ((), ())),
                                        preferred_element_type=F32)
    gin_v[0] = total.astype(BF16).reshape(rows, cols, chans)
    relay(3)
    pl.semaphore_signal(dp_sem, inc=1, device_id=device(z, lon, 1 - dp), device_id_type=MESH)

    for copy in a_copies:
        copy.wait_recv()
    for k in range(basis):
        summed = a_send[dp, q, k].astype(F32)
        for r in range(plane - 1):
            summed = summed + a_recv[r, k].astype(F32)
        b_send[k] = summed.astype(BF16)

    def keeper(k):
        return (FIRST_KEEPER + k) % nz

    for k in range(basis):
        @pl.when(z != keeper(k))
        def _(k=k):
            pltpu.make_async_remote_copy(
                src_ref=b_send.at[k], dst_ref=b_recv.at[z], send_sem=b_ssem.at[k],
                recv_sem=b_rsem.at[z], device_id=device(keeper(k), lon, dp),
                device_id_type=MESH).start()

    my_k = lax.rem(z + nz - FIRST_KEEPER % nz, nz)
    keeps = my_k < basis
    my_k = jnp.minimum(my_k, basis - 1)
    my_lanes = pl.ds(pl.multiple_of(dp * half, half), half)
    pl.semaphore_wait(dp_sem, 1)

    @pl.when(keeps)
    def _():
        for r in range(1, nz):
            place = lax.rem(z + r, nz)
            pltpu.make_async_copy(b_recv.at[place], b_recv.at[place], b_rsem.at[place]).wait()
        b_recv[z] = b_send[my_k]
        summed = jnp.zeros((blk, half), F32)
        for r in range(nz):
            summed = summed + b_recv[r].astype(F32)
        c_send[...] = (summed * scale).astype(BF16)
        for zz in range(nz):
            for dd in range(ndp):
                @pl.when(jnp.logical_or(z != zz, dp != dd))
                def _(zz=zz, dd=dd):
                    pltpu.make_async_remote_copy(
                        src_ref=c_send, dst_ref=final.at[my_k, :, my_lanes],
                        send_sem=c_ssem.at[dd * nz + zz], recv_sem=c_rsem.at[my_k * ndp + dp],
                        device_id=device(zz, lon, dd), device_id_type=MESH).start()
        final[my_k, :, my_lanes] = c_send[...]

    for k in range(basis):
        for h in range(ndp):
            @pl.when(jnp.logical_or(z != keeper(k), dp != h))
            def _(k=k, h=h):
                spot = final.at[k, :, pl.ds(h * half, half)]
                pltpu.make_async_copy(spot, spot, c_rsem.at[k * ndp + h]).wait()

    for copy in started:
        copy.wait_send()
    for copy in a_copies:
        copy.wait_send()
    for k in range(basis):
        @pl.when(z != keeper(k))
        def _(k=k):
            pltpu.make_async_copy(b_send.at[k], b_send.at[k], b_ssem.at[k]).wait()

    @pl.when(keeps)
    def _():
        for zz in range(nz):
            for dd in range(ndp):
                @pl.when(jnp.logical_or(z != zz, dp != dd))
                def _(zz=zz, dd=dd):
                    pltpu.make_async_copy(c_send, c_send, c_ssem.at[dd * nz + zz]).wait()


def hand_over(*refs):
    count = (len(refs) - 1) // 2
    copies = [pltpu.make_async_copy(refs[n], refs[count + n], refs[-1].at[n]) for n in range(count)]
    for copy in copies:
        copy.start()
    for copy in copies:
        copy.wait()


def on_device(input_field, cotangent, channel_weight, basis_filter, reach_cols):
    _, rows, cols, chans = input_field.shape
    basis, nlat, spans, taps = basis_filter.shape
    reach = taps // 2
    nz, nlon, ndp = (lax.axis_size(name) for name in ("lat", "lon", "dp"))
    nq = nlon // 2
    blk = chans // nlon
    block = cols + 2 * reach
    side = 2 * reach
    lanes = spans * block + side
    half = chans // ndp
    plane = nq * ndp

    first = lax.axis_index("lat") * rows
    offsets = jnp.abs(jnp.arange(taps, dtype=jnp.int32) - reach)
    inside = offsets[None, :] <= reach_cols[:, None]
    masked = jnp.where(inside[None, :, None, :], basis_filter, 0)
    near = lax.dynamic_slice_in_dim(jnp.pad(masked, ((0, 0), (1, 1), (0, 0), (0, 0))),
                                    first, rows + 2, 1)
    coeff = jnp.transpose(near, (2, 1, 0, 3))
    coeff = jnp.pad(coeff, ((0, 0), (0, 0), (0, 16 - basis), (0, 128 - taps)))
    coeff = coeff.reshape(spans, (rows + 2) * 16, 128).astype(BF16)

    sizes = (nz, nlon, ndp, basis, rows, cols, chans, taps)
    vmem = pl.BlockSpec(memory_space=pltpu.VMEM)
    hbm = pl.BlockSpec(memory_space=pltpu.HBM)
    dma = pltpu.SemaphoreType.DMA
    shapes = (jax.ShapeDtypeStruct(input_field.shape, BF16),
              jax.ShapeDtypeStruct(input_field.shape, BF16),
              jax.ShapeDtypeStruct((basis, blk, chans), BF16))
    results = pl.pallas_call(
        functools.partial(kernel_body, sizes),
        out_shape=shapes,
        in_specs=[vmem, hbm, hbm, hbm],
        out_specs=(vmem, vmem, vmem),
        scratch_shapes=[
            pltpu.VMEM((2, rows + 3, block, chans), BF16),
            pltpu.VMEM((2, rows + 2, side, chans), BF16),
            pltpu.VMEM((rows + 3, block, chans), BF16),
            pltpu.VMEM((2, rows + 2, side, chans), BF16),
            pltpu.VMEM((2, rows, cols, chans), BF16),
            pltpu.VMEM((basis, chans, chans), BF16),
            pltpu.VMEM((rows, basis * cols, lanes), BF16),
            pltpu.VMEM((rows, basis * cols, lanes), BF16),
            pltpu.VMEM((basis, 2 * rows, cols, chans), BF16),
            pltpu.VMEM((nq, 2, blk, 2 * rows * cols), BF16),
            pltpu.VMEM((ndp, nq, basis, blk, half), BF16),
            pltpu.VMEM((plane - 1, basis, blk, half), BF16),
            pltpu.VMEM((basis, blk, half), BF16),
            pltpu.VMEM((nz, blk, half), BF16),
            pltpu.VMEM((blk, half), BF16),
            dma((4,)), dma((19,)), dma((19,)), dma((plane - 1,)), dma((plane - 1,)),
            dma((basis,)), dma((nz,)), dma((nz * ndp,)), dma((basis * ndp,)),
            pltpu.SemaphoreType.REGULAR((4, 2)), pltpu.SemaphoreType.REGULAR,
        ],
        compiler_params=pltpu.CompilerParams(
            collective_id=0, has_side_effects=True),
        name="disco_block",
    )(coeff, input_field, cotangent, channel_weight)
    anywhere = pl.BlockSpec(memory_space=pl.ANY)
    out, gin, gw = pl.pallas_call(
        hand_over,
        out_shape=shapes,
        in_specs=[vmem] * 3,
        out_specs=(hbm, hbm, hbm),
        scratch_shapes=[dma((3,))],
        name="hand_over",
    )(*results)
    return out, gin, jnp.transpose(gw, (0, 2, 1))


def solution(mesh):
    placed = (P("dp", "lat", "lon", None), P("dp", "lat", "lon", None), P(), P(), P())
    return jax.shard_map(
        on_device,
        mesh=mesh,
        in_specs=placed,
        out_specs=(P("dp", "lat", "lon", None), P("dp", "lat", "lon", None), P(None, None, "lon")),
        check_vma=False,
    )
```

```python
import functools
import math

import jax
import jax.numpy as jnp
from jax import lax
from jax.experimental import pallas as pl
from jax.experimental.pallas import tpu as pltpu
from jax.sharding import PartitionSpec as P

MESH = pl.DeviceIdType.MESH
F32 = jnp.float32
BF16 = jnp.bfloat16


KEEPERS = (10, 11, 2, 12, 13, 1, 14, 15, 0)
GROUP = 3


def kernel_body(sizes, coeff_hbm, reach_hbm, field_hbm, cot_hbm, weight_hbm, out_hbm, gin_hbm,
                gw_hbm, coeff, reach_cols, out_v, gin_v, final, win, edge, cwin, cedge, cot, weight, fband, bband, conv, cot_t, a_send, a_recv,
                b_send, b_recv, c_send, local_sem, halo_send, halo_recv, a_ssem, a_rsem, b_ssem,
                b_rsem, c_ssem, c_rsem, near_sem, dp_sem):
    nz, nlon, ndp, nlat, basis, rows, cols, chans, taps = sizes
    reach = taps // 2
    nq = nlon // 2
    blk = chans // nlon
    scale = 1.0 / math.sqrt(ndp * nz * rows * nlon * cols)
    z = lax.axis_index("lat")
    lon = lax.axis_index("lon")
    dp = lax.axis_index("dp")
    q = lon // 2
    core = lon % 2
    mate = q * 2 + 1 - core
    block = cols + 2 * reach
    side = 2 * reach
    half = chans // ndp
    plane = nq * ndp

    def device(zz, ll, dd):
        return {"lat": zz, "lon": ll, "dp": dd}

    barrier = pltpu.get_barrier_semaphore()
    greeted = []

    def greet(*place):
        pl.semaphore_signal(barrier, inc=1, device_id=device(*place), device_id_type=MESH)
        greeted.append(place)

    up = lax.rem(z + 1, nz)
    down = lax.rem(z + nz - 1, nz)
    q_next = lax.rem(q + 1, nq)
    q_prev = lax.rem(q + nq - 1, nq)
    g = dp * nq + q
    for zz in (down, up):
        for cc in range(2):
            greet(zz, q * 2 + cc, dp)
    for zz in (down, up, z):
        greet(zz, q_prev * 2 + 1, dp)
        greet(zz, q_next * 2, dp)
    greet(z, mate, dp)
    for r in range(1, plane):
        place = lax.rem(g + r, plane)
        greet(z, lax.rem(place, nq) * 2 + core, place // nq)

    inside = (pl.ds(1, rows), pl.ds(side, cols))
    loads = [
        pltpu.make_async_copy(field_hbm.at[0], win.at[core, inside[0], inside[1]], local_sem.at[0]),
        pltpu.make_async_copy(cot_hbm.at[0], cot.at[core], local_sem.at[1]),
        pltpu.make_async_copy(cot_hbm.at[0], cwin.at[inside[0], inside[1]], local_sem.at[2]),
        pltpu.make_async_copy(weight_hbm, weight, local_sem.at[3]),
    ]
    small_loads = [
        pltpu.make_async_copy(coeff_hbm, coeff, local_sem.at[4]),
        pltpu.make_async_copy(reach_hbm, reach_cols, local_sem.at[5]),
    ]
    for load in small_loads + loads:
        load.start()

    pl.semaphore_wait(barrier, len(greeted))

    far = lax.rem(q + nq - 1 + 2 * core, nq)
    edge_cols = pl.ds(pl.multiple_of(core * (cols - side), 16), side)
    near_cols = pl.ds(pl.multiple_of((1 - core) * (cols - side), 16), side)
    started = []

    def send(src, dst, slots, zz, ll):
        copy = pltpu.make_async_remote_copy(
            src_ref=src, dst_ref=dst, send_sem=halo_send.at[slots[0]],
            recv_sem=halo_recv.at[slots[1]], device_id=device(zz, ll, dp), device_id_type=MESH)
        copy.start()
        started.append(copy)

    lat_sides = ((up, rows - 1, 0, 0), (down, 0, rows + 1, 1))
    for zz, row, place, which in lat_sides:
        for cc in range(2):
            send(field_hbm.at[0, row], win.at[core, place, inside[1]],
                 (which * 2 + cc, which * 2 + core), zz, q * 2 + cc)
    for zz, row, place, which in lat_sides:
        for cc in range(2):
            send(field_hbm.at[0, row, edge_cols], edge.at[1 - core, place],
                 (6 + which * 2 + cc, 6 + which * 2 + 1 - core), zz, far * 2 + cc)
    for cc in range(2):
        send(field_hbm.at[0, :, edge_cols], edge.at[1 - core, inside[0]],
             (4 + cc, 4 + 1 - core), z, far * 2 + cc)
    send(field_hbm.at[0], win.at[core, inside[0], inside[1]], (10, 10), z, mate)
    send(cot_hbm.at[0], cot.at[core], (11, 11), z, mate)
    for zz, row, place, which in lat_sides:
        send(cot_hbm.at[0, row], cwin.at[place, inside[1]], (12 + which, 12 + which), zz, lon)
        send(cot_hbm.at[0, row, near_cols], cedge.at[core, place], (14 + which, 14 + which),
             zz, mate)
        send(cot_hbm.at[0, row, edge_cols], cedge.at[1 - core, place], (16 + which, 16 + which),
             zz, far * 2 + 1 - core)
    send(cot_hbm.at[0, :, edge_cols], cedge.at[1 - core, inside[0]], (18, 18),
         z, far * 2 + 1 - core)

    def arrived(slot, like):
        pltpu.make_async_copy(like, like, halo_recv.at[slot]).wait()

    spans = []
    while 2 ** (len(spans) + 1) <= nz // 2:
        spans.append(2 ** len(spans))

    def tell(n):
        for way, step in ((0, spans[n]), (1, nz - spans[n])):
            pl.semaphore_signal(near_sem.at[n, way], inc=1,
                                device_id=device(lax.rem(z + step, nz), lon, dp),
                                device_id_type=MESH)

    def told(n):
        for way in range(2):
            pl.semaphore_wait(near_sem.at[n, way], 1)

    def relay(n):
        if 0 < n <= len(spans):
            told(n - 1)
        if n < len(spans):
            tell(n)

    relay(0)

    lanes = 3 * block + side
    tap_lane = lax.broadcasted_iota(jnp.int32, (taps, lanes), 0)
    out_lane = lax.broadcasted_iota(jnp.int32, (taps, lanes), 1)
    distance = jnp.abs(lax.broadcasted_iota(jnp.int32, (basis, taps), 1) - reach)
    first_row = z * rows
    held_row = jnp.clip(first_row - 1, 0, nlat - (rows + 2))

    def make_band(dst, transposed):
        for i in range(rows):
            rowvec = jnp.zeros((basis, lanes), F32)
            for a in range(3):
                if transposed:
                    row = jnp.clip(first_row + i - 1 + a, 0, nlat - 1)
                    picked = coeff[2 - a, row - held_row]
                    hit = out_lane == reach + block * a + (taps - 1) - tap_lane
                else:
                    row = first_row + i
                    picked = coeff[a, row - held_row]
                    hit = out_lane == reach + block * a + tap_lane
                picked = jnp.where(distance <= reach_cols[row], picked.astype(F32), 0.0)
                rowvec = rowvec + jnp.dot(picked.astype(BF16), jnp.where(hit, 1.0, 0.0).astype(BF16),
                                          preferred_element_type=F32)
            for k in range(basis):
                wide = jnp.broadcast_to(rowvec[k:k + 1, :], (cols, lanes))
                dst[i, pl.ds(k * cols, cols), :] = pltpu.roll(
                    wide, 0, 1, stride=1, stride_axis=0).astype(BF16)

    for load in small_loads:
        load.wait()
    make_band(fband, False)

    for load in loads:
        load.wait()
    arrived(11, cot.at[0])
    for s in range(2):
        for i in range(0, rows, 2):
            pair = cot[s, pl.ds(i, 2)].reshape(2 * cols, chans).astype(F32)
            cot_t[:, :, :, pl.ds((s * rows + i) * cols, 2 * cols)] = pair.T.astype(
                BF16).reshape(nq, 2, blk, 2 * cols)

    for slot in range(4):
        arrived(slot, win.at[0, 0, inside[1]])
    for slot in range(4, 6):
        arrived(slot, edge.at[0, inside[0]])
    for slot in range(6, 10):
        arrived(slot, edge.at[0, 0])
    arrived(10, win.at[0, inside[0], inside[1]])
    relay(1)

    def blank_field(place):
        for s in range(2):
            win[s, place, inside[1], :] = jnp.zeros((cols, chans), BF16)
            edge[s, place] = jnp.zeros((side, chans), BF16)

    @pl.when(z == 0)
    def _():
        blank_field(0)

    @pl.when(z == nz - 1)
    def _():
        blank_field(rows + 1)

    first_half = lax.broadcasted_iota(jnp.int32, (side, chans), 0) < reach
    nothing = jnp.zeros((side, chans), F32)

    def joint(before, after):
        before = nothing if before is None else before.astype(F32)
        after = nothing if after is None else after.astype(F32)
        return jnp.where(first_half, before, after).astype(BF16)

    for r in range(rows + 3):
        first, last = r == 0, r == rows + 2
        win[0, r, pl.ds(0, side), :] = joint(
            None if first else win[1, r - 1, pl.ds(side, side), :],
            None if last else edge[0, r])
        win[1, r, pl.ds(0, side), :] = joint(
            None if first else edge[1, r - 1],
            None if last else win[0, r, pl.ds(cols, side), :])

    for s in range(2):
        for i in range(rows):
            wide = jnp.concatenate([win[s, i], win[s, i + 1], win[s, i + 2],
                                    win[s, i + 3, pl.ds(0, side), :]], axis=0)
            part = jnp.dot(fband[i], wide, preferred_element_type=F32)
            conv[:, s * rows + i] = part.astype(BF16).reshape(basis, cols, chans)

    mine_t = cot_t[:, core].reshape(nq * blk, 2 * rows * cols)
    groups = [range(n, min(n + GROUP, basis)) for n in range(0, basis, GROUP)]
    a_copies = []
    for n, group in enumerate(groups):
        for k in group:
            terms = jnp.dot(mine_t, conv[k].reshape(2 * rows * cols, chans),
                            preferred_element_type=F32)
            terms = terms.astype(BF16).reshape(nq, blk, chans)
            for h in range(ndp):
                a_send[h, :, k] = terms[:, :, h * half:(h + 1) * half]
        part = pl.ds(group[0], len(group))
        copies = []
        for r in range(1, plane):
            place = lax.rem(g + r, plane)
            to_q = lax.rem(place, nq)
            copy = pltpu.make_async_remote_copy(
                src_ref=a_send.at[place // nq, to_q, part], dst_ref=a_recv.at[r - 1, part],
                send_sem=a_ssem.at[n, r - 1], recv_sem=a_rsem.at[n, r - 1],
                device_id=device(z, to_q * 2 + core, place // nq), device_id_type=MESH)
            copy.start()
            copies.append(copy)
        a_copies.append(copies)
    relay(2)

    make_band(bband, True)
    total = jnp.zeros((rows * cols, chans), F32)
    for k in range(basis):
        own = conv[k, pl.ds(core * rows, rows)].reshape(rows * cols, chans)
        total = total + jnp.dot(own, weight[k], preferred_element_type=F32)
    out_v[...] = total.astype(BF16).reshape(rows, cols, chans)
    out_copy = pltpu.make_async_copy(out_v, out_hbm.at[0], local_sem.at[0])
    out_copy.start()

    for slot in range(12, 14):
        arrived(slot, cwin.at[0, inside[1]])
    for slot in range(14, 18):
        arrived(slot, cedge.at[0, 0])
    arrived(18, cedge.at[0, inside[0]])
    cedge[1 - core, inside[0]] = cot[1 - core, :, edge_cols, :]

    def blank_cot(place):
        cwin[place, inside[1], :] = jnp.zeros((cols, chans), BF16)
        for s in range(2):
            cedge[s, place] = jnp.zeros((side, chans), BF16)

    @pl.when(z == 0)
    def _():
        blank_cot(0)

    @pl.when(z == nz - 1)
    def _():
        blank_cot(rows + 1)

    for r in range(rows + 3):
        cwin[r, pl.ds(0, side), :] = joint(
            None if r == 0 else cedge[1, r - 1], None if r == rows + 2 else cedge[0, r])
    for i in range(rows):
        wide = jnp.concatenate(
            [cwin[i], cwin[i + 1], cwin[i + 2], cwin[i + 3, pl.ds(0, side), :]], axis=0)
        part = jnp.dot(bband[i], wide, preferred_element_type=F32)
        conv[:, i] = part.astype(BF16).reshape(basis, cols, chans)
    total = jnp.zeros((rows * cols, chans), F32)
    for k in range(basis):
        own = conv[k, pl.ds(0, rows)].reshape(rows * cols, chans)
        total = total + lax.dot_general(own, weight[k], (((1,), (1,)), ((), ())),
                                        preferred_element_type=F32)
    gin_v[...] = total.astype(BF16).reshape(rows, cols, chans)
    gin_copy = pltpu.make_async_copy(gin_v, gin_hbm.at[0], local_sem.at[1])
    gin_copy.start()
    relay(3)
    pl.semaphore_signal(dp_sem, inc=1, device_id=device(z, lon, 1 - dp), device_id_type=MESH)

    def keeper(k):
        return KEEPERS[k] % nz

    for n, group in enumerate(groups):
        for copy in a_copies[n]:
            copy.wait_recv()
        for k in group:
            summed = a_send[dp, q, k].astype(F32)
            for r in range(plane - 1):
                summed = summed + a_recv[r, k].astype(F32)
            b_send[k] = summed.astype(BF16)

            @pl.when(z != keeper(k))
            def _(k=k):
                pltpu.make_async_remote_copy(
                    src_ref=b_send.at[k], dst_ref=b_recv.at[z], send_sem=b_ssem.at[k],
                    recv_sem=b_rsem.at[z], device_id=device(keeper(k), lon, dp),
                    device_id_type=MESH).start()

    my_k = jnp.int32(basis)
    for k in range(basis):
        my_k = jnp.where(z == keeper(k), k, my_k)
    keeps = my_k < basis
    my_k = jnp.minimum(my_k, basis - 1)
    my_lanes = pl.ds(pl.multiple_of(dp * half, half), half)
    pl.semaphore_wait(dp_sem, 1)

    @pl.when(keeps)
    def _():
        for r in range(1, nz):
            place = lax.rem(z + r, nz)
            pltpu.make_async_copy(b_recv.at[place], b_recv.at[place], b_rsem.at[place]).wait()
        b_recv[z] = b_send[my_k]
        summed = jnp.zeros((blk, half), F32)
        for r in range(nz):
            summed = summed + b_recv[r].astype(F32)
        c_send[...] = (summed * scale).astype(BF16)
        for zz in sorted(range(nz), key=lambda zz: (zz + nz // 2 + 1) % nz, reverse=True):
            for dd in range(ndp):
                @pl.when(jnp.logical_or(z != zz, dp != dd))
                def _(zz=zz, dd=dd):
                    pltpu.make_async_remote_copy(
                        src_ref=c_send, dst_ref=final.at[my_k, :, my_lanes],
                        send_sem=c_ssem.at[dd * nz + zz], recv_sem=c_rsem.at[my_k * ndp + dp],
                        device_id=device(zz, lon, dd), device_id_type=MESH).start()
        final[my_k, :, my_lanes] = c_send[...]

    for k in range(basis):
        for h in range(ndp):
            @pl.when(jnp.logical_or(z != keeper(k), dp != h))
            def _(k=k, h=h):
                spot = final.at[k, :, pl.ds(h * half, half)]
                pltpu.make_async_copy(spot, spot, c_rsem.at[k * ndp + h]).wait()

    gw_copy = pltpu.make_async_copy(final, gw_hbm, local_sem.at[2])
    gw_copy.start()

    for copy in started:
        copy.wait_send()
    for copies in a_copies:
        for copy in copies:
            copy.wait_send()
    for k in range(basis):
        @pl.when(z != keeper(k))
        def _(k=k):
            pltpu.make_async_copy(b_send.at[k], b_send.at[k], b_ssem.at[k]).wait()

    @pl.when(keeps)
    def _():
        for zz in range(nz):
            for dd in range(ndp):
                @pl.when(jnp.logical_or(z != zz, dp != dd))
                def _(zz=zz, dd=dd):
                    pltpu.make_async_copy(c_send, c_send, c_ssem.at[dd * nz + zz]).wait()

    out_copy.wait()
    gin_copy.wait()
    gw_copy.wait()


def hand_over(*refs):
    count = (len(refs) - 1) // 2
    copies = [pltpu.make_async_copy(refs[n], refs[count + n], refs[-1].at[n]) for n in range(count)]
    for copy in copies:
        copy.start()
    for copy in copies:
        copy.wait()


def on_device(input_field, cotangent, channel_weight, basis_filter, reach_cols):
    _, rows, cols, chans = input_field.shape
    basis, nlat, spans, taps = basis_filter.shape
    reach = taps // 2
    groups = pl.cdiv(basis, GROUP)
    nz, nlon, ndp = (lax.axis_size(name) for name in ("lat", "lon", "dp"))
    nq = nlon // 2
    blk = chans // nlon
    block = cols + 2 * reach
    side = 2 * reach
    lanes = spans * block + side
    half = chans // ndp
    plane = nq * ndp

    first = lax.axis_index("lat") * rows
    start = jnp.clip(first - 1, 0, nlat - (rows + 2))
    coeff = jnp.transpose(lax.dynamic_slice_in_dim(basis_filter, start, rows + 2, 1), (2, 1, 0, 3))
    sizes = (nz, nlon, ndp, nlat, basis, rows, cols, chans, taps)
    vmem = pl.BlockSpec(memory_space=pltpu.VMEM)
    hbm = pl.BlockSpec(memory_space=pltpu.HBM)
    dma = pltpu.SemaphoreType.DMA
    shapes = (jax.ShapeDtypeStruct(input_field.shape, BF16),
              jax.ShapeDtypeStruct(input_field.shape, BF16),
              jax.ShapeDtypeStruct((basis, blk, chans), BF16))
    results = pl.pallas_call(
        functools.partial(kernel_body, sizes),
        out_shape=shapes,
        in_specs=[hbm] * 5,
        out_specs=(hbm, hbm, hbm),
        scratch_shapes=[
            pltpu.VMEM((spans, rows + 2, basis, taps), BF16),
            pltpu.SMEM((nlat,), jnp.int32),
            pltpu.VMEM((rows, cols, chans), BF16),
            pltpu.VMEM((rows, cols, chans), BF16),
            pltpu.VMEM((basis, blk, chans), BF16),
            pltpu.VMEM((2, rows + 3, block, chans), BF16),
            pltpu.VMEM((2, rows + 2, side, chans), BF16),
            pltpu.VMEM((rows + 3, block, chans), BF16),
            pltpu.VMEM((2, rows + 2, side, chans), BF16),
            pltpu.VMEM((2, rows, cols, chans), BF16),
            pltpu.VMEM((basis, chans, chans), BF16),
            pltpu.VMEM((rows, basis * cols, lanes), BF16),
            pltpu.VMEM((rows, basis * cols, lanes), BF16),
            pltpu.VMEM((basis, 2 * rows, cols, chans), BF16),
            pltpu.VMEM((nq, 2, blk, 2 * rows * cols), BF16),
            pltpu.VMEM((ndp, nq, basis, blk, half), BF16),
            pltpu.VMEM((plane - 1, basis, blk, half), BF16),
            pltpu.VMEM((basis, blk, half), BF16),
            pltpu.VMEM((nz, blk, half), BF16),
            pltpu.VMEM((blk, half), BF16),
            dma((6,)), dma((19,)), dma((19,)), dma((groups, plane - 1)), dma((groups, plane - 1)),
            dma((basis,)), dma((nz,)), dma((nz * ndp,)), dma((basis * ndp,)),
            pltpu.SemaphoreType.REGULAR((4, 2)), pltpu.SemaphoreType.REGULAR,
        ],
        compiler_params=pltpu.CompilerParams(
            collective_id=0, has_side_effects=True),
        name="disco_block",
    )(coeff, reach_cols, input_field, cotangent, channel_weight)
    anywhere = pl.BlockSpec(memory_space=pl.ANY)
    out, gin, gw = pl.pallas_call(
        hand_over,
        out_shape=shapes,
        in_specs=[vmem] * 3,
        out_specs=(hbm, hbm, hbm),
        scratch_shapes=[dma((3,))],
        name="hand_over",
    )(*results)
    return out, gin, jnp.transpose(gw, (0, 2, 1))


def solution(mesh):
    placed = (P("dp", "lat", "lon", None), P("dp", "lat", "lon", None), P(), P(), P())
    return jax.shard_map(
        on_device,
        mesh=mesh,
        in_specs=placed,
        out_specs=(P("dp", "lat", "lon", None), P("dp", "lat", "lon", None), P(None, None, "lon")),
        check_vma=False,
    )
```

```python
import functools
import math

import jax
import jax.numpy as jnp
from jax import lax
from jax.experimental import pallas as pl
from jax.experimental.pallas import tpu as pltpu
from jax.sharding import PartitionSpec as P

MESH = pl.DeviceIdType.MESH
F32 = jnp.float32
BF16 = jnp.bfloat16


KEEPERS = (12, 3, 11, 13, 2, 14, 15, 1, 0)
GROUP = 3


def kernel_body(sizes, coeff_hbm, reach_hbm, field_hbm, cot_hbm, weight_hbm, out_hbm, gin_hbm,
                gw_hbm, coeff, reach_cols, out_v, gin_v, final, win, edge, cwin, cedge, cot, weight, fband, bband, conv, cot_t, a_send, a_recv,
                b_send, b_recv, c_send, local_sem, halo_send, halo_recv, a_ssem, a_rsem, b_ssem,
                b_rsem, c_ssem, c_rsem, near_sem, plane_sem,
                dp_sem):
    nz, nlon, ndp, nlat, basis, rows, cols, chans, taps = sizes
    reach = taps // 2
    nq = nlon // 2
    blk = chans // nlon
    scale = 1.0 / math.sqrt(ndp * nz * rows * nlon * cols)
    z = lax.axis_index("lat")
    lon = lax.axis_index("lon")
    dp = lax.axis_index("dp")
    q = lon // 2
    core = lon % 2
    mate = q * 2 + 1 - core
    block = cols + 2 * reach
    side = 2 * reach
    half = chans // ndp
    plane = nq * ndp

    def device(zz, ll, dd):
        return {"lat": zz, "lon": ll, "dp": dd}

    inside = (pl.ds(1, rows), pl.ds(side, cols))
    loads = [
        pltpu.make_async_copy(field_hbm.at[0], win.at[core, inside[0], inside[1]], local_sem.at[0]),
        pltpu.make_async_copy(cot_hbm.at[0], cot.at[core], local_sem.at[1]),
        pltpu.make_async_copy(cot_hbm.at[0], cwin.at[inside[0], inside[1]], local_sem.at[2]),
        pltpu.make_async_copy(weight_hbm, weight, local_sem.at[3]),
    ]
    small_loads = [
        pltpu.make_async_copy(coeff_hbm, coeff, local_sem.at[4]),
        pltpu.make_async_copy(reach_hbm, reach_cols, local_sem.at[5]),
    ]
    for load in small_loads + loads:
        load.start()

    barrier = pltpu.get_barrier_semaphore()
    greeted = []

    def greet(*place):
        pl.semaphore_signal(barrier, inc=1, device_id=device(*place), device_id_type=MESH)
        greeted.append(place)

    up = lax.rem(z + 1, nz)
    down = lax.rem(z + nz - 1, nz)
    q_next = lax.rem(q + 1, nq)
    q_prev = lax.rem(q + nq - 1, nq)
    g = dp * nq + q
    for zz in (down, up):
        for cc in range(2):
            greet(zz, q * 2 + cc, dp)
    for zz in (down, up, z):
        greet(zz, q_prev * 2 + 1, dp)
        greet(zz, q_next * 2, dp)
    greet(z, mate, dp)
    ny = 2 * ndp
    nx = plane // ny

    def in_plane(dx, dy):
        xx = lax.rem(q // 2 + dx, nx)
        yy = lax.rem(dp * 2 + q % 2 + dy, ny)
        return z, (xx * 2 + yy % 2) * 2 + core, yy // 2

    steps = ((1, 0), (nx - 1, 0), (0, 1), (0, ny - 1))
    for step in steps:
        greet(*in_plane(*step))

    pl.semaphore_wait(barrier, len(greeted))
    for load in loads[:2]:
        load.wait()

    far = lax.rem(q + nq - 1 + 2 * core, nq)
    edge_cols = pl.ds(pl.multiple_of(core * (cols - side), 16), side)
    near_cols = pl.ds(pl.multiple_of((1 - core) * (cols - side), 16), side)
    win_cols = pl.ds(pl.multiple_of(side + core * (cols - side), 16), side)
    started = []

    def send(src, dst, slots, zz, ll):
        copy = pltpu.make_async_remote_copy(
            src_ref=src, dst_ref=dst, send_sem=halo_send.at[slots[0]],
            recv_sem=halo_recv.at[slots[1]], device_id=device(zz, ll, dp), device_id_type=MESH)
        copy.start()
        started.append(copy)

    lat_sides = ((up, rows - 1, 0, 0), (down, 0, rows + 1, 1))
    for zz, row, place, which in lat_sides:
        for cc in range(2):
            send(win.at[core, row + 1, inside[1]], win.at[core, place, inside[1]],
                 (which * 2 + cc, which * 2 + core), zz, q * 2 + cc)
    for zz, row, place, which in lat_sides:
        for cc in range(2):
            send(win.at[core, row + 1, win_cols], edge.at[1 - core, place],
                 (6 + which * 2 + cc, 6 + which * 2 + 1 - core), zz, far * 2 + cc)
    for cc in range(2):
        send(win.at[core, inside[0], win_cols], edge.at[1 - core, inside[0]],
             (4 + cc, 4 + 1 - core), z, far * 2 + cc)
    own = win.at[core, inside[0], inside[1]]
    send(own, own, (10, 10), z, mate)
    send(cot.at[core], cot.at[core], (11, 11), z, mate)
    for zz, row, place, which in lat_sides:
        send(cot.at[core, row], cwin.at[place, inside[1]], (12 + which, 12 + which), zz, lon)
        send(cot.at[core, row, near_cols], cedge.at[core, place], (14 + which, 14 + which),
             zz, mate)
        send(cot.at[core, row, edge_cols], cedge.at[1 - core, place], (16 + which, 16 + which),
             zz, far * 2 + 1 - core)
    send(cot.at[core, :, edge_cols], cedge.at[1 - core, inside[0]], (18, 18),
         z, far * 2 + 1 - core)

    def arrived(slot, like):
        pltpu.make_async_copy(like, like, halo_recv.at[slot]).wait()

    spans = []
    while 2 ** (len(spans) + 1) <= nz // 2:
        spans.append(2 ** len(spans))

    def tell(n):
        for way, step in ((0, spans[n]), (1, nz - spans[n])):
            pl.semaphore_signal(near_sem.at[n, way], inc=1,
                                device_id=device(lax.rem(z + step, nz), lon, dp),
                                device_id_type=MESH)

    def told(n):
        for way in range(2):
            pl.semaphore_wait(near_sem.at[n, way], 1)

    def tell_plane(far_steps, base):
        for n, step in enumerate(far_steps):
            pl.semaphore_signal(plane_sem.at[base + n], inc=1, device_id=device(*in_plane(*step)),
                                device_id_type=MESH)

    def told_plane(far_steps, base):
        for n in range(len(far_steps)):
            pl.semaphore_wait(plane_sem.at[base + n], 1)

    jumps = [step for step, size in (((2, 0), nx), ((0, 2), ny)) if size > 2]

    def relay(n):
        if 0 < n <= len(spans):
            told(n - 1)
        if n < len(spans):
            tell(n)

    relay(0)
    tell_plane(steps, 0)

    lanes = 3 * block + side
    tap_lane = lax.broadcasted_iota(jnp.int32, (taps, lanes), 0)
    out_lane = lax.broadcasted_iota(jnp.int32, (taps, lanes), 1)
    distance = jnp.abs(lax.broadcasted_iota(jnp.int32, (basis, taps), 1) - reach)
    first_row = z * rows
    held_row = jnp.clip(first_row - 1, 0, nlat - (rows + 2))

    def make_band(dst, transposed):
        for i in range(rows):
            rowvec = jnp.zeros((basis, lanes), F32)
            for a in range(3):
                if transposed:
                    row = jnp.clip(first_row + i - 1 + a, 0, nlat - 1)
                    picked = coeff[2 - a, row - held_row]
                    hit = out_lane == reach + block * a + (taps - 1) - tap_lane
                else:
                    row = first_row + i
                    picked = coeff[a, row - held_row]
                    hit = out_lane == reach + block * a + tap_lane
                picked = jnp.where(distance <= reach_cols[row], picked.astype(F32), 0.0)
                rowvec = rowvec + jnp.dot(picked.astype(BF16), jnp.where(hit, 1.0, 0.0).astype(BF16),
                                          preferred_element_type=F32)
            for k in range(basis):
                wide = jnp.broadcast_to(rowvec[k:k + 1, :], (cols, lanes))
                dst[i, pl.ds(k * cols, cols), :] = pltpu.roll(
                    wide, 0, 1, stride=1, stride_axis=0).astype(BF16)

    for load in small_loads:
        load.wait()
    make_band(fband, False)
    told_plane(steps, 0)
    tell_plane(jumps, len(steps))

    for load in loads[2:]:
        load.wait()
    arrived(11, cot.at[0])
    for s in range(2):
        for i in range(0, rows, 2):
            pair = cot[s, pl.ds(i, 2)].reshape(2 * cols, chans).astype(F32)
            cot_t[:, :, :, pl.ds((s * rows + i) * cols, 2 * cols)] = pair.T.astype(
                BF16).reshape(nq, 2, blk, 2 * cols)

    for slot in range(4):
        arrived(slot, win.at[0, 0, inside[1]])
    for slot in range(4, 6):
        arrived(slot, edge.at[0, inside[0]])
    for slot in range(6, 10):
        arrived(slot, edge.at[0, 0])
    arrived(10, win.at[0, inside[0], inside[1]])
    relay(1)

    def blank_field(place):
        for s in range(2):
            win[s, place, inside[1], :] = jnp.zeros((cols, chans), BF16)
            edge[s, place] = jnp.zeros((side, chans), BF16)

    @pl.when(z == 0)
    def _():
        blank_field(0)

    @pl.when(z == nz - 1)
    def _():
        blank_field(rows + 1)

    first_half = lax.broadcasted_iota(jnp.int32, (side, chans), 0) < reach
    nothing = jnp.zeros((side, chans), F32)

    def joint(before, after):
        before = nothing if before is None else before.astype(F32)
        after = nothing if after is None else after.astype(F32)
        return jnp.where(first_half, before, after).astype(BF16)

    for r in range(rows + 3):
        first, last = r == 0, r == rows + 2
        win[0, r, pl.ds(0, side), :] = joint(
            None if first else win[1, r - 1, pl.ds(side, side), :],
            None if last else edge[0, r])
        win[1, r, pl.ds(0, side), :] = joint(
            None if first else edge[1, r - 1],
            None if last else win[0, r, pl.ds(cols, side), :])

    for s in range(2):
        for i in range(rows):
            wide = jnp.concatenate([win[s, i], win[s, i + 1], win[s, i + 2],
                                    win[s, i + 3, pl.ds(0, side), :]], axis=0)
            part = jnp.dot(fband[i], wide, preferred_element_type=F32)
            conv[:, s * rows + i] = part.astype(BF16).reshape(basis, cols, chans)

    mine_t = cot_t[:, core].reshape(nq * blk, 2 * rows * cols)
    told_plane(jumps, len(steps))
    groups = [range(n, min(n + GROUP, basis)) for n in range(0, basis, GROUP)]
    a_copies = []
    for n, group in enumerate(groups):
        for k in group:
            terms = jnp.dot(mine_t, conv[k].reshape(2 * rows * cols, chans),
                            preferred_element_type=F32)
            terms = terms.astype(BF16).reshape(nq, blk, chans)
            for h in range(ndp):
                a_send[h, :, k] = terms[:, :, h * half:(h + 1) * half]
        part = pl.ds(group[0], len(group))
        copies = []
        for r in range(1, plane):
            place = lax.rem(g + r, plane)
            to_q = lax.rem(place, nq)
            copy = pltpu.make_async_remote_copy(
                src_ref=a_send.at[place // nq, to_q, part], dst_ref=a_recv.at[r - 1, part],
                send_sem=a_ssem.at[n, r - 1], recv_sem=a_rsem.at[n, r - 1],
                device_id=device(z, to_q * 2 + core, place // nq), device_id_type=MESH)
            copy.start()
            copies.append(copy)
        a_copies.append(copies)
    relay(2)

    make_band(bband, True)
    total = jnp.zeros((rows * cols, chans), F32)
    for k in range(basis):
        own = conv[k, pl.ds(core * rows, rows)].reshape(rows * cols, chans)
        total = total + jnp.dot(own, weight[k], preferred_element_type=F32)
    out_v[...] = total.astype(BF16).reshape(rows, cols, chans)
    out_copy = pltpu.make_async_copy(out_v, out_hbm.at[0], local_sem.at[0])
    out_copy.start()

    for slot in range(12, 14):
        arrived(slot, cwin.at[0, inside[1]])
    for slot in range(14, 18):
        arrived(slot, cedge.at[0, 0])
    arrived(18, cedge.at[0, inside[0]])
    cedge[1 - core, inside[0]] = cot[1 - core, :, edge_cols, :]

    def blank_cot(place):
        cwin[place, inside[1], :] = jnp.zeros((cols, chans), BF16)
        for s in range(2):
            cedge[s, place] = jnp.zeros((side, chans), BF16)

    @pl.when(z == 0)
    def _():
        blank_cot(0)

    @pl.when(z == nz - 1)
    def _():
        blank_cot(rows + 1)

    for r in range(rows + 3):
        cwin[r, pl.ds(0, side), :] = joint(
            None if r == 0 else cedge[1, r - 1], None if r == rows + 2 else cedge[0, r])
    for i in range(rows):
        wide = jnp.concatenate(
            [cwin[i], cwin[i + 1], cwin[i + 2], cwin[i + 3, pl.ds(0, side), :]], axis=0)
        part = jnp.dot(bband[i], wide, preferred_element_type=F32)
        conv[:, i] = part.astype(BF16).reshape(basis, cols, chans)
    total = jnp.zeros((rows * cols, chans), F32)
    for k in range(basis):
        own = conv[k, pl.ds(0, rows)].reshape(rows * cols, chans)
        total = total + lax.dot_general(own, weight[k], (((1,), (1,)), ((), ())),
                                        preferred_element_type=F32)
    gin_v[...] = total.astype(BF16).reshape(rows, cols, chans)
    gin_copy = pltpu.make_async_copy(gin_v, gin_hbm.at[0], local_sem.at[1])
    gin_copy.start()
    relay(3)
    pl.semaphore_signal(dp_sem, inc=1, device_id=device(z, lon, 1 - dp), device_id_type=MESH)

    def keeper(k):
        return KEEPERS[k] % nz

    for n, group in enumerate(groups):
        for copy in a_copies[n]:
            copy.wait_recv()
        for k in group:
            summed = a_send[dp, q, k].astype(F32)
            for r in range(plane - 1):
                summed = summed + a_recv[r, k].astype(F32)
            b_send[k] = summed.astype(BF16)

            @pl.when(z != keeper(k))
            def _(k=k):
                pltpu.make_async_remote_copy(
                    src_ref=b_send.at[k], dst_ref=b_recv.at[z], send_sem=b_ssem.at[k],
                    recv_sem=b_rsem.at[z], device_id=device(keeper(k), lon, dp),
                    device_id_type=MESH).start()

    for copy in started:
        copy.wait_send()
    for copies in a_copies:
        for copy in copies:
            copy.wait_send()
    for k in range(basis):
        @pl.when(z != keeper(k))
        def _(k=k):
            pltpu.make_async_copy(b_send.at[k], b_send.at[k], b_ssem.at[k]).wait()

    my_k = jnp.int32(basis)
    for k in range(basis):
        my_k = jnp.where(z == keeper(k), k, my_k)
    keeps = my_k < basis
    my_k = jnp.minimum(my_k, basis - 1)
    my_lanes = pl.ds(pl.multiple_of(dp * half, half), half)
    pl.semaphore_wait(dp_sem, 1)

    @pl.when(keeps)
    def _():
        for r in range(1, nz):
            place = lax.rem(z + r, nz)
            pltpu.make_async_copy(b_recv.at[place], b_recv.at[place], b_rsem.at[place]).wait()
        b_recv[z] = b_send[my_k]
        summed = jnp.zeros((blk, half), F32)
        for r in range(nz):
            summed = summed + b_recv[r].astype(F32)
        c_send[...] = (summed * scale).astype(BF16)
        for zz in range(nz):
            for dd in range(ndp):
                @pl.when(jnp.logical_or(z != zz, dp != dd))
                def _(zz=zz, dd=dd):
                    pltpu.make_async_remote_copy(
                        src_ref=c_send, dst_ref=final.at[my_k, :, my_lanes],
                        send_sem=c_ssem.at[dd * nz + zz], recv_sem=c_rsem.at[my_k * ndp + dp],
                        device_id=device(zz, lon, dd), device_id_type=MESH).start()
        final[my_k, :, my_lanes] = c_send[...]

    for k in range(basis):
        for h in range(ndp):
            @pl.when(jnp.logical_or(z != keeper(k), dp != h))
            def _(k=k, h=h):
                spot = final.at[k, :, pl.ds(h * half, half)]
                pltpu.make_async_copy(spot, spot, c_rsem.at[k * ndp + h]).wait()

    gw_copy = pltpu.make_async_copy(final, gw_hbm, local_sem.at[2])
    gw_copy.start()

    @pl.when(keeps)
    def _():
        for zz in range(nz):
            for dd in range(ndp):
                @pl.when(jnp.logical_or(z != zz, dp != dd))
                def _(zz=zz, dd=dd):
                    pltpu.make_async_copy(c_send, c_send, c_ssem.at[dd * nz + zz]).wait()

    out_copy.wait()
    gin_copy.wait()
    gw_copy.wait()


def hand_over(*refs):
    count = (len(refs) - 1) // 2
    copies = [pltpu.make_async_copy(refs[n], refs[count + n], refs[-1].at[n]) for n in range(count)]
    for copy in copies:
        copy.start()
    for copy in copies:
        copy.wait()


def on_device(input_field, cotangent, channel_weight, basis_filter, reach_cols):
    _, rows, cols, chans = input_field.shape
    basis, nlat, spans, taps = basis_filter.shape
    reach = taps // 2
    groups = pl.cdiv(basis, GROUP)
    nz, nlon, ndp = (lax.axis_size(name) for name in ("lat", "lon", "dp"))
    nq = nlon // 2
    blk = chans // nlon
    block = cols + 2 * reach
    side = 2 * reach
    lanes = spans * block + side
    half = chans // ndp
    plane = nq * ndp

    first = lax.axis_index("lat") * rows
    start = jnp.clip(first - 1, 0, nlat - (rows + 2))
    coeff = jnp.transpose(lax.dynamic_slice_in_dim(basis_filter, start, rows + 2, 1), (2, 1, 0, 3))
    sizes = (nz, nlon, ndp, nlat, basis, rows, cols, chans, taps)
    vmem = pl.BlockSpec(memory_space=pltpu.VMEM)
    hbm = pl.BlockSpec(memory_space=pltpu.HBM)
    dma = pltpu.SemaphoreType.DMA
    shapes = (jax.ShapeDtypeStruct(input_field.shape, BF16),
              jax.ShapeDtypeStruct(input_field.shape, BF16),
              jax.ShapeDtypeStruct((basis, blk, chans), BF16))
    results = pl.pallas_call(
        functools.partial(kernel_body, sizes),
        out_shape=shapes,
        in_specs=[hbm] * 5,
        out_specs=(hbm, hbm, hbm),
        scratch_shapes=[
            pltpu.VMEM((spans, rows + 2, basis, taps), BF16),
            pltpu.SMEM((nlat,), jnp.int32),
            pltpu.VMEM((rows, cols, chans), BF16),
            pltpu.VMEM((rows, cols, chans), BF16),
            pltpu.VMEM((basis, blk, chans), BF16),
            pltpu.VMEM((2, rows + 3, block, chans), BF16),
            pltpu.VMEM((2, rows + 2, side, chans), BF16),
            pltpu.VMEM((rows + 3, block, chans), BF16),
            pltpu.VMEM((2, rows + 2, side, chans), BF16),
            pltpu.VMEM((2, rows, cols, chans), BF16),
            pltpu.VMEM((basis, chans, chans), BF16),
            pltpu.VMEM((rows, basis * cols, lanes), BF16),
            pltpu.VMEM((rows, basis * cols, lanes), BF16),
            pltpu.VMEM((basis, 2 * rows, cols, chans), BF16),
            pltpu.VMEM((nq, 2, blk, 2 * rows * cols), BF16),
            pltpu.VMEM((ndp, nq, basis, blk, half), BF16),
            pltpu.VMEM((plane - 1, basis, blk, half), BF16),
            pltpu.VMEM((basis, blk, half), BF16),
            pltpu.VMEM((nz, blk, half), BF16),
            pltpu.VMEM((blk, half), BF16),
            dma((6,)), dma((19,)), dma((19,)), dma((groups, plane - 1)), dma((groups, plane - 1)),
            dma((basis,)), dma((nz,)), dma((nz * ndp,)), dma((basis * ndp,)),
            pltpu.SemaphoreType.REGULAR((4, 2)), pltpu.SemaphoreType.REGULAR((6,)),
            pltpu.SemaphoreType.REGULAR,
        ],
        compiler_params=pltpu.CompilerParams(
            collective_id=0, has_side_effects=True),
        name="disco_block",
    )(coeff, reach_cols, input_field, cotangent, channel_weight)
    anywhere = pl.BlockSpec(memory_space=pl.ANY)
    out, gin, gw = pl.pallas_call(
        hand_over,
        out_shape=shapes,
        in_specs=[vmem] * 3,
        out_specs=(hbm, hbm, hbm),
        scratch_shapes=[dma((3,))],
        name="hand_over",
    )(*results)
    return out, gin, jnp.transpose(gw, (0, 2, 1))


def solution(mesh):
    placed = (P("dp", "lat", "lon", None), P("dp", "lat", "lon", None), P(), P(), P())
    return jax.shard_map(
        on_device,
        mesh=mesh,
        in_specs=placed,
        out_specs=(P("dp", "lat", "lon", None), P("dp", "lat", "lon", None), P(None, None, "lon")),
        check_vma=False,
    )
```

```python
import functools
import math

import jax
import jax.numpy as jnp
from jax import lax
from jax.experimental import pallas as pl
from jax.experimental.pallas import tpu as pltpu
from jax.sharding import PartitionSpec as P

MESH = pl.DeviceIdType.MESH
F32 = jnp.float32
BF16 = jnp.bfloat16


KEEPERS = (12, 3, 11, 13, 2, 14, 15, 1, 0)
GROUP = 3


def kernel_body(sizes, coeff_hbm, reach_hbm, field_hbm, cot_hbm, weight_hbm, out_hbm, gin_hbm,
                gw_hbm, coeff, reach_cols, out_v, gin_v, final, win, edge, cwin, cedge, cot, weight, fband, bband, conv, cot_t, a_send, a_recv,
                b_send, b_recv, c_send, local_sem, halo_send, halo_recv, a_ssem, a_rsem, b_ssem,
                b_rsem, c_ssem, c_rsem, near_sem, plane_sem,
                dp_sem):
    nz, nlon, ndp, nlat, basis, rows, cols, chans, taps = sizes
    reach = taps // 2
    nq = nlon // 2
    blk = chans // nlon
    scale = 1.0 / math.sqrt(ndp * nz * rows * nlon * cols)
    z = lax.axis_index("lat")
    lon = lax.axis_index("lon")
    dp = lax.axis_index("dp")
    q = lon // 2
    core = lon % 2
    mate = q * 2 + 1 - core
    block = cols + 2 * reach
    side = 2 * reach
    half = chans // ndp
    plane = nq * ndp

    def device(zz, ll, dd):
        return {"lat": zz, "lon": ll, "dp": dd}

    inside = (pl.ds(1, rows), pl.ds(side, cols))
    loads = [
        pltpu.make_async_copy(field_hbm.at[0], win.at[core, inside[0], inside[1]], local_sem.at[0]),
        pltpu.make_async_copy(cot_hbm.at[0], cot.at[core], local_sem.at[1]),
        pltpu.make_async_copy(cot_hbm.at[0], cwin.at[inside[0], inside[1]], local_sem.at[2]),
        pltpu.make_async_copy(weight_hbm, weight, local_sem.at[3]),
    ]
    small_loads = [
        pltpu.make_async_copy(coeff_hbm, coeff, local_sem.at[4]),
        pltpu.make_async_copy(reach_hbm, reach_cols, local_sem.at[5]),
    ]
    for load in small_loads + loads:
        load.start()

    barrier = pltpu.get_barrier_semaphore()
    greeted = []

    def greet(*place):
        pl.semaphore_signal(barrier, inc=1, device_id=device(*place), device_id_type=MESH)
        greeted.append(place)

    up = lax.rem(z + 1, nz)
    down = lax.rem(z + nz - 1, nz)
    q_next = lax.rem(q + 1, nq)
    q_prev = lax.rem(q + nq - 1, nq)
    g = dp * nq + q
    for zz in (down, up):
        for cc in range(2):
            greet(zz, q * 2 + cc, dp)
    for zz in (down, up, z):
        greet(zz, q_prev * 2 + 1, dp)
        greet(zz, q_next * 2, dp)
    greet(z, mate, dp)
    ny = 2 * ndp
    nx = plane // ny

    def in_plane(dx, dy):
        xx = lax.rem(q // 2 + dx, nx)
        yy = lax.rem(dp * 2 + q % 2 + dy, ny)
        return z, (xx * 2 + yy % 2) * 2 + core, yy // 2

    steps = ((1, 0), (nx - 1, 0), (0, 1), (0, ny - 1))
    for step in steps:
        greet(*in_plane(*step))

    pl.semaphore_wait(barrier, len(greeted))
    for load in loads[:2]:
        load.wait()

    far = lax.rem(q + nq - 1 + 2 * core, nq)
    edge_cols = pl.ds(pl.multiple_of(core * (cols - side), 16), side)
    near_cols = pl.ds(pl.multiple_of((1 - core) * (cols - side), 16), side)
    win_cols = pl.ds(pl.multiple_of(side + core * (cols - side), 16), side)
    started = []

    def send(src, dst, slots, zz, ll):
        copy = pltpu.make_async_remote_copy(
            src_ref=src, dst_ref=dst, send_sem=halo_send.at[slots[0]],
            recv_sem=halo_recv.at[slots[1]], device_id=device(zz, ll, dp), device_id_type=MESH)
        copy.start()
        started.append(copy)

    lat_sides = ((up, rows - 1, 0, 0), (down, 0, rows + 1, 1))
    for zz, row, place, which in lat_sides:
        for cc in range(2):
            send(win.at[core, row + 1, win_cols], edge.at[1 - core, place],
                 (6 + which * 2 + cc, 6 + which * 2 + 1 - core), zz, far * 2 + cc)
    for cc in range(2):
        send(win.at[core, inside[0], win_cols], edge.at[1 - core, inside[0]],
             (4 + cc, 4 + 1 - core), z, far * 2 + cc)
    for zz, row, place, which in lat_sides:
        for cc in range(2):
            send(win.at[core, row + 1, inside[1]], win.at[core, place, inside[1]],
                 (which * 2 + cc, which * 2 + core), zz, q * 2 + cc)
    own = win.at[core, inside[0], inside[1]]
    send(own, own, (10, 10), z, mate)
    send(cot.at[core], cot.at[core], (11, 11), z, mate)
    for zz, row, place, which in lat_sides:
        send(cot.at[core, row], cwin.at[place, inside[1]], (12 + which, 12 + which), zz, lon)
        send(cot.at[core, row, near_cols], cedge.at[core, place], (14 + which, 14 + which),
             zz, mate)
        send(cot.at[core, row, edge_cols], cedge.at[1 - core, place], (16 + which, 16 + which),
             zz, far * 2 + 1 - core)
    send(cot.at[core, :, edge_cols], cedge.at[1 - core, inside[0]], (18, 18),
         z, far * 2 + 1 - core)

    def arrived(slot, like):
        pltpu.make_async_copy(like, like, halo_recv.at[slot]).wait()

    spans = []
    while 2 ** (len(spans) + 1) <= nz // 2:
        spans.append(2 ** len(spans))

    def tell(n):
        for way, step in ((0, spans[n]), (1, nz - spans[n])):
            pl.semaphore_signal(near_sem.at[n, way], inc=1,
                                device_id=device(lax.rem(z + step, nz), lon, dp),
                                device_id_type=MESH)

    def told(n):
        for way in range(2):
            pl.semaphore_wait(near_sem.at[n, way], 1)

    def tell_plane(far_steps, base):
        for n, step in enumerate(far_steps):
            pl.semaphore_signal(plane_sem.at[base + n], inc=1, device_id=device(*in_plane(*step)),
                                device_id_type=MESH)

    def told_plane(far_steps, base):
        for n in range(len(far_steps)):
            pl.semaphore_wait(plane_sem.at[base + n], 1)

    jumps = [step for step, size in (((2, 0), nx), ((0, 2), ny)) if size > 2]

    def relay(n):
        if 0 < n <= len(spans):
            told(n - 1)
        if n < len(spans):
            tell(n)

    relay(0)
    tell_plane(steps, 0)

    lanes = 3 * block + side
    tap_lane = lax.broadcasted_iota(jnp.int32, (taps, lanes), 0)
    out_lane = lax.broadcasted_iota(jnp.int32, (taps, lanes), 1)
    distance = jnp.abs(lax.broadcasted_iota(jnp.int32, (basis, taps), 1) - reach)
    first_row = z * rows
    held_row = jnp.clip(first_row - 1, 0, nlat - (rows + 2))

    def make_band(dst, transposed):
        for i in range(rows):
            rowvec = jnp.zeros((basis, lanes), F32)
            for a in range(3):
                if transposed:
                    row = jnp.clip(first_row + i - 1 + a, 0, nlat - 1)
                    picked = coeff[2 - a, row - held_row]
                    hit = out_lane == reach + block * a + (taps - 1) - tap_lane
                else:
                    row = first_row + i
                    picked = coeff[a, row - held_row]
                    hit = out_lane == reach + block * a + tap_lane
                picked = jnp.where(distance <= reach_cols[row], picked.astype(F32), 0.0)
                rowvec = rowvec + jnp.dot(picked.astype(BF16), jnp.where(hit, 1.0, 0.0).astype(BF16),
                                          preferred_element_type=F32)
            for k in range(basis):
                wide = jnp.broadcast_to(rowvec[k:k + 1, :], (cols, lanes))
                dst[i, pl.ds(k * cols, cols), :] = pltpu.roll(
                    wide, 0, 1, stride=1, stride_axis=0).astype(BF16)

    for load in small_loads:
        load.wait()
    make_band(fband, False)
    told_plane(steps, 0)
    tell_plane(jumps, len(steps))

    for load in loads[2:]:
        load.wait()
    arrived(11, cot.at[0])
    for s in range(2):
        for i in range(0, rows, 2):
            pair = cot[s, pl.ds(i, 2)].reshape(2 * cols, chans).astype(F32)
            cot_t[:, :, :, pl.ds((s * rows + i) * cols, 2 * cols)] = pair.T.astype(
                BF16).reshape(nq, 2, blk, 2 * cols)

    for slot in range(4):
        arrived(slot, win.at[0, 0, inside[1]])
    for slot in range(4, 6):
        arrived(slot, edge.at[0, inside[0]])
    for slot in range(6, 10):
        arrived(slot, edge.at[0, 0])
    arrived(10, win.at[0, inside[0], inside[1]])
    relay(1)

    def blank_field(place):
        for s in range(2):
            win[s, place, inside[1], :] = jnp.zeros((cols, chans), BF16)
            edge[s, place] = jnp.zeros((side, chans), BF16)

    @pl.when(z == 0)
    def _():
        blank_field(0)

    @pl.when(z == nz - 1)
    def _():
        blank_field(rows + 1)

    first_half = lax.broadcasted_iota(jnp.int32, (side, chans), 0) < reach
    nothing = jnp.zeros((side, chans), F32)

    def joint(before, after):
        before = nothing if before is None else before.astype(F32)
        after = nothing if after is None else after.astype(F32)
        return jnp.where(first_half, before, after).astype(BF16)

    for r in range(rows + 3):
        first, last = r == 0, r == rows + 2
        win[0, r, pl.ds(0, side), :] = joint(
            None if first else win[1, r - 1, pl.ds(side, side), :],
            None if last else edge[0, r])
        win[1, r, pl.ds(0, side), :] = joint(
            None if first else edge[1, r - 1],
            None if last else win[0, r, pl.ds(cols, side), :])

    for s in range(2):
        for i in range(rows):
            wide = jnp.concatenate([win[s, i], win[s, i + 1], win[s, i + 2],
                                    win[s, i + 3, pl.ds(0, side), :]], axis=0)
            part = jnp.dot(fband[i], wide, preferred_element_type=F32)
            conv[:, s * rows + i] = part.astype(BF16).reshape(basis, cols, chans)

    mine_t = cot_t[:, core].reshape(nq * blk, 2 * rows * cols)
    told_plane(jumps, len(steps))
    groups = [range(n, min(n + GROUP, basis)) for n in range(0, basis, GROUP)]
    a_copies = []
    for n, group in enumerate(groups):
        for k in group:
            terms = jnp.dot(mine_t, conv[k].reshape(2 * rows * cols, chans),
                            preferred_element_type=F32)
            terms = terms.astype(BF16).reshape(nq, blk, chans)
            for h in range(ndp):
                a_send[h, :, k] = terms[:, :, h * half:(h + 1) * half]
        part = pl.ds(group[0], len(group))
        copies = []
        for r in range(1, plane):
            place = lax.rem(g + r, plane)
            to_q = lax.rem(place, nq)
            copy = pltpu.make_async_remote_copy(
                src_ref=a_send.at[place // nq, to_q, part], dst_ref=a_recv.at[r - 1, part],
                send_sem=a_ssem.at[n, r - 1], recv_sem=a_rsem.at[n, r - 1],
                device_id=device(z, to_q * 2 + core, place // nq), device_id_type=MESH)
            copy.start()
            copies.append(copy)
        a_copies.append(copies)
    relay(2)

    make_band(bband, True)
    total = jnp.zeros((rows * cols, chans), F32)
    for k in range(basis):
        own = conv[k, pl.ds(core * rows, rows)].reshape(rows * cols, chans)
        total = total + jnp.dot(own, weight[k], preferred_element_type=F32)
    out_v[...] = total.astype(BF16).reshape(rows, cols, chans)
    out_copy = pltpu.make_async_copy(out_v, out_hbm.at[0], local_sem.at[0])
    out_copy.start()

    for slot in range(12, 14):
        arrived(slot, cwin.at[0, inside[1]])
    for slot in range(14, 18):
        arrived(slot, cedge.at[0, 0])
    arrived(18, cedge.at[0, inside[0]])
    cedge[1 - core, inside[0]] = cot[1 - core, :, edge_cols, :]

    def blank_cot(place):
        cwin[place, inside[1], :] = jnp.zeros((cols, chans), BF16)
        for s in range(2):
            cedge[s, place] = jnp.zeros((side, chans), BF16)

    @pl.when(z == 0)
    def _():
        blank_cot(0)

    @pl.when(z == nz - 1)
    def _():
        blank_cot(rows + 1)

    for r in range(rows + 3):
        cwin[r, pl.ds(0, side), :] = joint(
            None if r == 0 else cedge[1, r - 1], None if r == rows + 2 else cedge[0, r])
    for i in range(rows):
        wide = jnp.concatenate(
            [cwin[i], cwin[i + 1], cwin[i + 2], cwin[i + 3, pl.ds(0, side), :]], axis=0)
        part = jnp.dot(bband[i], wide, preferred_element_type=F32)
        conv[:, i] = part.astype(BF16).reshape(basis, cols, chans)
    total = jnp.zeros((rows * cols, chans), F32)
    for k in range(basis):
        own = conv[k, pl.ds(0, rows)].reshape(rows * cols, chans)
        total = total + lax.dot_general(own, weight[k], (((1,), (1,)), ((), ())),
                                        preferred_element_type=F32)
    gin_v[...] = total.astype(BF16).reshape(rows, cols, chans)
    gin_copy = pltpu.make_async_copy(gin_v, gin_hbm.at[0], local_sem.at[1])
    gin_copy.start()
    relay(3)
    pl.semaphore_signal(dp_sem, inc=1, device_id=device(z, lon, 1 - dp), device_id_type=MESH)

    def keeper(k):
        return KEEPERS[k] % nz

    for n, group in enumerate(groups):
        for copy in a_copies[n]:
            copy.wait_recv()
        for k in group:
            summed = a_send[dp, q, k].astype(F32)
            for r in range(plane - 1):
                summed = summed + a_recv[r, k].astype(F32)
            b_send[k] = summed.astype(BF16)

            @pl.when(z != keeper(k))
            def _(k=k):
                pltpu.make_async_remote_copy(
                    src_ref=b_send.at[k], dst_ref=b_recv.at[z], send_sem=b_ssem.at[k],
                    recv_sem=b_rsem.at[z], device_id=device(keeper(k), lon, dp),
                    device_id_type=MESH).start()

    for copy in started:
        copy.wait_send()
    for copies in a_copies:
        for copy in copies:
            copy.wait_send()
    for k in range(basis):
        @pl.when(z != keeper(k))
        def _(k=k):
            pltpu.make_async_copy(b_send.at[k], b_send.at[k], b_ssem.at[k]).wait()

    my_k = jnp.int32(basis)
    for k in range(basis):
        my_k = jnp.where(z == keeper(k), k, my_k)
    keeps = my_k < basis
    my_k = jnp.minimum(my_k, basis - 1)
    my_lanes = pl.ds(pl.multiple_of(dp * half, half), half)
    pl.semaphore_wait(dp_sem, 1)

    @pl.when(keeps)
    def _():
        for r in range(1, nz):
            place = lax.rem(z + r, nz)
            pltpu.make_async_copy(b_recv.at[place], b_recv.at[place], b_rsem.at[place]).wait()
        b_recv[z] = b_send[my_k]
        summed = jnp.zeros((blk, half), F32)
        for r in range(nz):
            summed = summed + b_recv[r].astype(F32)
        c_send[...] = (summed * scale).astype(BF16)
        for zz in range(nz):
            for dd in [(dp + 1 + n) % ndp for n in range(ndp)]:
                @pl.when(jnp.logical_or(z != zz, dp != dd))
                def _(zz=zz, dd=dd):
                    pltpu.make_async_remote_copy(
                        src_ref=c_send, dst_ref=final.at[my_k, :, my_lanes],
                        send_sem=c_ssem.at[dd * nz + zz], recv_sem=c_rsem.at[my_k * ndp + dp],
                        device_id=device(zz, lon, dd), device_id_type=MESH).start()
        final[my_k, :, my_lanes] = c_send[...]

    for k in range(basis):
        for h in range(ndp):
            @pl.when(jnp.logical_or(z != keeper(k), dp != h))
            def _(k=k, h=h):
                spot = final.at[k, :, pl.ds(h * half, half)]
                pltpu.make_async_copy(spot, spot, c_rsem.at[k * ndp + h]).wait()

    gw_copy = pltpu.make_async_copy(final, gw_hbm, local_sem.at[2])
    gw_copy.start()

    @pl.when(keeps)
    def _():
        for zz in range(nz):
            for dd in range(ndp):
                @pl.when(jnp.logical_or(z != zz, dp != dd))
                def _(zz=zz, dd=dd):
                    pltpu.make_async_copy(c_send, c_send, c_ssem.at[dd * nz + zz]).wait()

    out_copy.wait()
    gin_copy.wait()
    gw_copy.wait()


def hand_over(*refs):
    count = (len(refs) - 1) // 2
    copies = [pltpu.make_async_copy(refs[n], refs[count + n], refs[-1].at[n]) for n in range(count)]
    for copy in copies:
        copy.start()
    for copy in copies:
        copy.wait()


def on_device(input_field, cotangent, channel_weight, basis_filter, reach_cols):
    _, rows, cols, chans = input_field.shape
    basis, nlat, spans, taps = basis_filter.shape
    reach = taps // 2
    groups = pl.cdiv(basis, GROUP)
    nz, nlon, ndp = (lax.axis_size(name) for name in ("lat", "lon", "dp"))
    nq = nlon // 2
    blk = chans // nlon
    block = cols + 2 * reach
    side = 2 * reach
    lanes = spans * block + side
    half = chans // ndp
    plane = nq * ndp

    first = lax.axis_index("lat") * rows
    start = jnp.clip(first - 1, 0, nlat - (rows + 2))
    coeff = jnp.transpose(lax.dynamic_slice_in_dim(basis_filter, start, rows + 2, 1), (2, 1, 0, 3))
    sizes = (nz, nlon, ndp, nlat, basis, rows, cols, chans, taps)
    vmem = pl.BlockSpec(memory_space=pltpu.VMEM)
    hbm = pl.BlockSpec(memory_space=pltpu.HBM)
    dma = pltpu.SemaphoreType.DMA
    shapes = (jax.ShapeDtypeStruct(input_field.shape, BF16),
              jax.ShapeDtypeStruct(input_field.shape, BF16),
              jax.ShapeDtypeStruct((basis, blk, chans), BF16))
    results = pl.pallas_call(
        functools.partial(kernel_body, sizes),
        out_shape=shapes,
        in_specs=[hbm] * 5,
        out_specs=(hbm, hbm, hbm),
        scratch_shapes=[
            pltpu.VMEM((spans, rows + 2, basis, taps), BF16),
            pltpu.SMEM((nlat,), jnp.int32),
            pltpu.VMEM((rows, cols, chans), BF16),
            pltpu.VMEM((rows, cols, chans), BF16),
            pltpu.VMEM((basis, blk, chans), BF16),
            pltpu.VMEM((2, rows + 3, block, chans), BF16),
            pltpu.VMEM((2, rows + 2, side, chans), BF16),
            pltpu.VMEM((rows + 3, block, chans), BF16),
            pltpu.VMEM((2, rows + 2, side, chans), BF16),
            pltpu.VMEM((2, rows, cols, chans), BF16),
            pltpu.VMEM((basis, chans, chans), BF16),
            pltpu.VMEM((rows, basis * cols, lanes), BF16),
            pltpu.VMEM((rows, basis * cols, lanes), BF16),
            pltpu.VMEM((basis, 2 * rows, cols, chans), BF16),
            pltpu.VMEM((nq, 2, blk, 2 * rows * cols), BF16),
            pltpu.VMEM((ndp, nq, basis, blk, half), BF16),
            pltpu.VMEM((plane - 1, basis, blk, half), BF16),
            pltpu.VMEM((basis, blk, half), BF16),
            pltpu.VMEM((nz, blk, half), BF16),
            pltpu.VMEM((blk, half), BF16),
            dma((6,)), dma((19,)), dma((19,)), dma((groups, plane - 1)), dma((groups, plane - 1)),
            dma((basis,)), dma((nz,)), dma((nz * ndp,)), dma((basis * ndp,)),
            pltpu.SemaphoreType.REGULAR((4, 2)), pltpu.SemaphoreType.REGULAR((6,)),
            pltpu.SemaphoreType.REGULAR,
        ],
        compiler_params=pltpu.CompilerParams(
            collective_id=0, has_side_effects=True),
        name="disco_block",
    )(coeff, reach_cols, input_field, cotangent, channel_weight)
    anywhere = pl.BlockSpec(memory_space=pl.ANY)
    out, gin, gw = pl.pallas_call(
        hand_over,
        out_shape=shapes,
        in_specs=[vmem] * 3,
        out_specs=(hbm, hbm, hbm),
        scratch_shapes=[dma((3,))],
        name="hand_over",
    )(*results)
    return out, gin, jnp.transpose(gw, (0, 2, 1))


def solution(mesh):
    placed = (P("dp", "lat", "lon", None), P("dp", "lat", "lon", None), P(), P(), P())
    return jax.shard_map(
        on_device,
        mesh=mesh,
        in_specs=placed,
        out_specs=(P("dp", "lat", "lon", None), P("dp", "lat", "lon", None), P(None, None, "lon")),
        check_vma=False,
    )
```

```python
import functools
import math

import jax
import jax.numpy as jnp
from jax import lax
from jax.experimental import pallas as pl
from jax.experimental.pallas import tpu as pltpu
from jax.sharding import PartitionSpec as P

MESH = pl.DeviceIdType.MESH
F32 = jnp.float32
BF16 = jnp.bfloat16


KEEPERS = (12, 3, 11, 13, 2, 14, 15, 1, 0)
GROUP = 3


def kernel_body(sizes, coeff_hbm, reach_hbm, field_hbm, cot_hbm, weight_hbm, out_hbm, gin_hbm,
                gw_hbm, coeff, reach_cols, out_v, gin_v, final, win, edge, cwin, cedge, cot, weight, fband, bband, conv, cot_t, a_send, a_recv,
                b_send, b_recv, c_send, local_sem, halo_send, halo_recv, a_ssem, a_rsem, b_ssem,
                b_rsem, c_ssem, c_rsem, near_sem, plane_sem,
                dp_sem):
    nz, nlon, ndp, nlat, basis, rows, cols, chans, taps = sizes
    reach = taps // 2
    nq = nlon // 2
    blk = chans // nlon
    scale = 1.0 / math.sqrt(ndp * nz * rows * nlon * cols)
    z = lax.axis_index("lat")
    lon = lax.axis_index("lon")
    dp = lax.axis_index("dp")
    q = lon // 2
    core = lon % 2
    mate = q * 2 + 1 - core
    block = cols + 2 * reach
    side = 2 * reach
    half = chans // ndp
    plane = nq * ndp

    def device(zz, ll, dd):
        return {"lat": zz, "lon": ll, "dp": dd}

    barrier = pltpu.get_barrier_semaphore()
    greeted = []

    def greet(*place):
        pl.semaphore_signal(barrier, inc=1, device_id=device(*place), device_id_type=MESH)
        greeted.append(place)

    up = lax.rem(z + 1, nz)
    down = lax.rem(z + nz - 1, nz)
    q_next = lax.rem(q + 1, nq)
    q_prev = lax.rem(q + nq - 1, nq)
    g = dp * nq + q
    for zz in (down, up):
        for cc in range(2):
            greet(zz, q * 2 + cc, dp)
    for zz in (down, up, z):
        greet(zz, q_prev * 2 + 1, dp)
        greet(zz, q_next * 2, dp)
    greet(z, mate, dp)
    ny = 2 * ndp
    nx = plane // ny

    def in_plane(dx, dy):
        xx = lax.rem(q // 2 + dx, nx)
        yy = lax.rem(dp * 2 + q % 2 + dy, ny)
        return z, (xx * 2 + yy % 2) * 2 + core, yy // 2

    steps = ((1, 0), (nx - 1, 0), (0, 1), (0, ny - 1))
    for step in steps:
        greet(*in_plane(*step))

    inside = (pl.ds(1, rows), pl.ds(side, cols))
    loads = [
        pltpu.make_async_copy(field_hbm.at[0], win.at[core, inside[0], inside[1]], local_sem.at[0]),
        pltpu.make_async_copy(cot_hbm.at[0], cot.at[core], local_sem.at[1]),
        pltpu.make_async_copy(cot_hbm.at[0], cwin.at[inside[0], inside[1]], local_sem.at[2]),
        pltpu.make_async_copy(weight_hbm, weight, local_sem.at[3]),
    ]
    small_loads = [
        pltpu.make_async_copy(coeff_hbm, coeff, local_sem.at[4]),
        pltpu.make_async_copy(reach_hbm, reach_cols, local_sem.at[5]),
    ]
    for load in loads[:2] + small_loads + loads[2:3]:
        load.start()

    pl.semaphore_wait(barrier, len(greeted))
    for load in loads[:2]:
        load.wait()

    far = lax.rem(q + nq - 1 + 2 * core, nq)
    edge_cols = pl.ds(pl.multiple_of(core * (cols - side), 16), side)
    near_cols = pl.ds(pl.multiple_of((1 - core) * (cols - side), 16), side)
    win_cols = pl.ds(pl.multiple_of(side + core * (cols - side), 16), side)
    started = []

    def send(src, dst, slots, zz, ll):
        copy = pltpu.make_async_remote_copy(
            src_ref=src, dst_ref=dst, send_sem=halo_send.at[slots[0]],
            recv_sem=halo_recv.at[slots[1]], device_id=device(zz, ll, dp), device_id_type=MESH)
        copy.start()
        started.append(copy)

    lat_sides = ((up, rows - 1, 0, 0), (down, 0, rows + 1, 1))
    for zz, row, place, which in lat_sides:
        for cc in range(2):
            send(win.at[core, row + 1, win_cols], edge.at[1 - core, place],
                 (6 + which * 2 + cc, 6 + which * 2 + 1 - core), zz, far * 2 + cc)
    for cc in range(2):
        send(win.at[core, inside[0], win_cols], edge.at[1 - core, inside[0]],
             (4 + cc, 4 + 1 - core), z, far * 2 + cc)
    for zz, row, place, which in lat_sides:
        for cc in range(2):
            send(win.at[core, row + 1, inside[1]], win.at[core, place, inside[1]],
                 (which * 2 + cc, which * 2 + core), zz, q * 2 + cc)
    own = win.at[core, inside[0], inside[1]]
    send(own, own, (10, 10), z, mate)
    send(cot.at[core], cot.at[core], (11, 11), z, mate)
    for zz, row, place, which in lat_sides:
        send(cot.at[core, row], cwin.at[place, inside[1]], (12 + which, 12 + which), zz, lon)
        send(cot.at[core, row, near_cols], cedge.at[core, place], (14 + which, 14 + which),
             zz, mate)
        send(cot.at[core, row, edge_cols], cedge.at[1 - core, place], (16 + which, 16 + which),
             zz, far * 2 + 1 - core)
    send(cot.at[core, :, edge_cols], cedge.at[1 - core, inside[0]], (18, 18),
         z, far * 2 + 1 - core)

    def arrived(slot, like):
        pltpu.make_async_copy(like, like, halo_recv.at[slot]).wait()

    spans = []
    while 2 ** (len(spans) + 1) <= nz // 2:
        spans.append(2 ** len(spans))

    def tell(n):
        for way, step in ((0, spans[n]), (1, nz - spans[n])):
            pl.semaphore_signal(near_sem.at[n, way], inc=1,
                                device_id=device(lax.rem(z + step, nz), lon, dp),
                                device_id_type=MESH)

    def told(n):
        for way in range(2):
            pl.semaphore_wait(near_sem.at[n, way], 1)

    def tell_plane(far_steps, base):
        for n, step in enumerate(far_steps):
            pl.semaphore_signal(plane_sem.at[base + n], inc=1, device_id=device(*in_plane(*step)),
                                device_id_type=MESH)

    def told_plane(far_steps, base):
        for n in range(len(far_steps)):
            pl.semaphore_wait(plane_sem.at[base + n], 1)

    jumps = [step for step, size in (((2, 0), nx), ((0, 2), ny)) if size > 2]

    def relay(n):
        if 0 < n <= len(spans):
            told(n - 1)
        if n < len(spans):
            tell(n)

    loads[3].start()
    relay(0)
    tell_plane(steps, 0)

    lanes = 3 * block + side
    tap_lane = lax.broadcasted_iota(jnp.int32, (taps, lanes), 0)
    out_lane = lax.broadcasted_iota(jnp.int32, (taps, lanes), 1)
    distance = jnp.abs(lax.broadcasted_iota(jnp.int32, (basis, taps), 1) - reach)
    first_row = z * rows
    held_row = jnp.clip(first_row - 1, 0, nlat - (rows + 2))

    def make_band(dst, transposed):
        for i in range(rows):
            rowvec = jnp.zeros((basis, lanes), F32)
            for a in range(3):
                if transposed:
                    row = jnp.clip(first_row + i - 1 + a, 0, nlat - 1)
                    picked = coeff[2 - a, row - held_row]
                    hit = out_lane == reach + block * a + (taps - 1) - tap_lane
                else:
                    row = first_row + i
                    picked = coeff[a, row - held_row]
                    hit = out_lane == reach + block * a + tap_lane
                picked = jnp.where(distance <= reach_cols[row], picked.astype(F32), 0.0)
                rowvec = rowvec + jnp.dot(picked.astype(BF16), jnp.where(hit, 1.0, 0.0).astype(BF16),
                                          preferred_element_type=F32)
            for k in range(basis):
                wide = jnp.broadcast_to(rowvec[k:k + 1, :], (cols, lanes))
                dst[i, pl.ds(k * cols, cols), :] = pltpu.roll(
                    wide, 0, 1, stride=1, stride_axis=0).astype(BF16)

    for load in small_loads:
        load.wait()
    make_band(fband, False)
    told_plane(steps, 0)
    tell_plane(jumps, len(steps))

    for load in loads[2:]:
        load.wait()
    arrived(11, cot.at[0])
    for s in range(2):
        for i in range(0, rows, 2):
            pair = cot[s, pl.ds(i, 2)].reshape(2 * cols, chans).astype(F32)
            cot_t[:, :, :, pl.ds((s * rows + i) * cols, 2 * cols)] = pair.T.astype(
                BF16).reshape(nq, 2, blk, 2 * cols)

    for slot in range(4):
        arrived(slot, win.at[0, 0, inside[1]])
    for slot in range(4, 6):
        arrived(slot, edge.at[0, inside[0]])
    for slot in range(6, 10):
        arrived(slot, edge.at[0, 0])
    arrived(10, win.at[0, inside[0], inside[1]])
    relay(1)

    def blank_field(place):
        for s in range(2):
            win[s, place, inside[1], :] = jnp.zeros((cols, chans), BF16)
            edge[s, place] = jnp.zeros((side, chans), BF16)

    @pl.when(z == 0)
    def _():
        blank_field(0)

    @pl.when(z == nz - 1)
    def _():
        blank_field(rows + 1)

    first_half = lax.broadcasted_iota(jnp.int32, (side, chans), 0) < reach
    nothing = jnp.zeros((side, chans), F32)

    def joint(before, after):
        before = nothing if before is None else before.astype(F32)
        after = nothing if after is None else after.astype(F32)
        return jnp.where(first_half, before, after).astype(BF16)

    for r in range(rows + 3):
        first, last = r == 0, r == rows + 2
        win[0, r, pl.ds(0, side), :] = joint(
            None if first else win[1, r - 1, pl.ds(side, side), :],
            None if last else edge[0, r])
        win[1, r, pl.ds(0, side), :] = joint(
            None if first else edge[1, r - 1],
            None if last else win[0, r, pl.ds(cols, side), :])

    for s in range(2):
        for i in range(rows):
            wide = jnp.concatenate([win[s, i], win[s, i + 1], win[s, i + 2],
                                    win[s, i + 3, pl.ds(0, side), :]], axis=0)
            part = jnp.dot(fband[i], wide, preferred_element_type=F32)
            conv[:, s * rows + i] = part.astype(BF16).reshape(basis, cols, chans)

    mine_t = cot_t[:, core].reshape(nq * blk, 2 * rows * cols)
    told_plane(jumps, len(steps))
    groups = [range(n, min(n + GROUP, basis)) for n in range(0, basis, GROUP)]
    a_copies = []
    for n, group in enumerate(groups):
        for k in group:
            terms = jnp.dot(mine_t, conv[k].reshape(2 * rows * cols, chans),
                            preferred_element_type=F32)
            terms = terms.astype(BF16).reshape(nq, blk, chans)
            for h in range(ndp):
                a_send[h, :, k] = terms[:, :, h * half:(h + 1) * half]
        part = pl.ds(group[0], len(group))
        copies = []
        for r in range(1, plane):
            place = lax.rem(g + r, plane)
            to_q = lax.rem(place, nq)
            copy = pltpu.make_async_remote_copy(
                src_ref=a_send.at[place // nq, to_q, part], dst_ref=a_recv.at[r - 1, part],
                send_sem=a_ssem.at[n, r - 1], recv_sem=a_rsem.at[n, r - 1],
                device_id=device(z, to_q * 2 + core, place // nq), device_id_type=MESH)
            copy.start()
            copies.append(copy)
        a_copies.append(copies)
    relay(2)

    make_band(bband, True)
    total = jnp.zeros((rows * cols, chans), F32)
    for k in range(basis):
        own = conv[k, pl.ds(core * rows, rows)].reshape(rows * cols, chans)
        total = total + jnp.dot(own, weight[k], preferred_element_type=F32)
    out_v[...] = total.astype(BF16).reshape(rows, cols, chans)
    out_copy = pltpu.make_async_copy(out_v, out_hbm.at[0], local_sem.at[0])
    out_copy.start()

    for slot in range(12, 14):
        arrived(slot, cwin.at[0, inside[1]])
    for slot in range(14, 18):
        arrived(slot, cedge.at[0, 0])
    arrived(18, cedge.at[0, inside[0]])
    cedge[1 - core, inside[0]] = cot[1 - core, :, edge_cols, :]

    def blank_cot(place):
        cwin[place, inside[1], :] = jnp.zeros((cols, chans), BF16)
        for s in range(2):
            cedge[s, place] = jnp.zeros((side, chans), BF16)

    @pl.when(z == 0)
    def _():
        blank_cot(0)

    @pl.when(z == nz - 1)
    def _():
        blank_cot(rows + 1)

    for r in range(rows + 3):
        cwin[r, pl.ds(0, side), :] = joint(
            None if r == 0 else cedge[1, r - 1], None if r == rows + 2 else cedge[0, r])
    for i in range(rows):
        wide = jnp.concatenate(
            [cwin[i], cwin[i + 1], cwin[i + 2], cwin[i + 3, pl.ds(0, side), :]], axis=0)
        part = jnp.dot(bband[i], wide, preferred_element_type=F32)
        conv[:, i] = part.astype(BF16).reshape(basis, cols, chans)
    total = jnp.zeros((rows * cols, chans), F32)
    for k in range(basis):
        own = conv[k, pl.ds(0, rows)].reshape(rows * cols, chans)
        total = total + lax.dot_general(own, weight[k], (((1,), (1,)), ((), ())),
                                        preferred_element_type=F32)
    gin_v[...] = total.astype(BF16).reshape(rows, cols, chans)
    gin_copy = pltpu.make_async_copy(gin_v, gin_hbm.at[0], local_sem.at[1])
    gin_copy.start()
    relay(3)
    pl.semaphore_signal(dp_sem, inc=1, device_id=device(z, lon, 1 - dp), device_id_type=MESH)

    def keeper(k):
        return KEEPERS[k] % nz

    for n, group in enumerate(groups):
        for copy in a_copies[n]:
            copy.wait_recv()
        for k in group:
            summed = a_send[dp, q, k].astype(F32)
            for r in range(plane - 1):
                summed = summed + a_recv[r, k].astype(F32)
            b_send[k] = summed.astype(BF16)

            @pl.when(z != keeper(k))
            def _(k=k):
                pltpu.make_async_remote_copy(
                    src_ref=b_send.at[k], dst_ref=b_recv.at[z], send_sem=b_ssem.at[k],
                    recv_sem=b_rsem.at[z], device_id=device(keeper(k), lon, dp),
                    device_id_type=MESH).start()

    for copy in started:
        copy.wait_send()
    for copies in a_copies:
        for copy in copies:
            copy.wait_send()
    for k in range(basis):
        @pl.when(z != keeper(k))
        def _(k=k):
            pltpu.make_async_copy(b_send.at[k], b_send.at[k], b_ssem.at[k]).wait()

    my_k = jnp.int32(basis)
    for k in range(basis):
        my_k = jnp.where(z == keeper(k), k, my_k)
    keeps = my_k < basis
    my_k = jnp.minimum(my_k, basis - 1)
    my_lanes = pl.ds(pl.multiple_of(dp * half, half), half)
    pl.semaphore_wait(dp_sem, 1)

    @pl.when(keeps)
    def _():
        for r in range(1, nz):
            place = lax.rem(z + r, nz)
            pltpu.make_async_copy(b_recv.at[place], b_recv.at[place], b_rsem.at[place]).wait()
        b_recv[z] = b_send[my_k]
        summed = jnp.zeros((blk, half), F32)
        for r in range(nz):
            summed = summed + b_recv[r].astype(F32)
        c_send[...] = (summed * scale).astype(BF16)
        for zz in range(nz):
            for dd in [(dp + 1 + n) % ndp for n in range(ndp)]:
                @pl.when(jnp.logical_or(z != zz, dp != dd))
                def _(zz=zz, dd=dd):
                    pltpu.make_async_remote_copy(
                        src_ref=c_send, dst_ref=final.at[my_k, :, my_lanes],
                        send_sem=c_ssem.at[dd * nz + zz], recv_sem=c_rsem.at[my_k * ndp + dp],
                        device_id=device(zz, lon, dd), device_id_type=MESH).start()
        final[my_k, :, my_lanes] = c_send[...]

    for k in range(basis):
        for h in range(ndp):
            @pl.when(jnp.logical_or(z != keeper(k), dp != h))
            def _(k=k, h=h):
                spot = final.at[k, :, pl.ds(h * half, half)]
                pltpu.make_async_copy(spot, spot, c_rsem.at[k * ndp + h]).wait()

    gw_copy = pltpu.make_async_copy(final, gw_hbm, local_sem.at[2])
    gw_copy.start()

    @pl.when(keeps)
    def _():
        for zz in range(nz):
            for dd in range(ndp):
                @pl.when(jnp.logical_or(z != zz, dp != dd))
                def _(zz=zz, dd=dd):
                    pltpu.make_async_copy(c_send, c_send, c_ssem.at[dd * nz + zz]).wait()

    out_copy.wait()
    gin_copy.wait()
    gw_copy.wait()


def hand_over(*refs):
    count = (len(refs) - 1) // 2
    copies = [pltpu.make_async_copy(refs[n], refs[count + n], refs[-1].at[n]) for n in range(count)]
    for copy in copies:
        copy.start()
    for copy in copies:
        copy.wait()


def on_device(input_field, cotangent, channel_weight, basis_filter, reach_cols):
    _, rows, cols, chans = input_field.shape
    basis, nlat, spans, taps = basis_filter.shape
    reach = taps // 2
    groups = pl.cdiv(basis, GROUP)
    nz, nlon, ndp = (lax.axis_size(name) for name in ("lat", "lon", "dp"))
    nq = nlon // 2
    blk = chans // nlon
    block = cols + 2 * reach
    side = 2 * reach
    lanes = spans * block + side
    half = chans // ndp
    plane = nq * ndp

    first = lax.axis_index("lat") * rows
    start = jnp.clip(first - 1, 0, nlat - (rows + 2))
    coeff = jnp.transpose(lax.dynamic_slice_in_dim(basis_filter, start, rows + 2, 1), (2, 1, 0, 3))
    sizes = (nz, nlon, ndp, nlat, basis, rows, cols, chans, taps)
    vmem = pl.BlockSpec(memory_space=pltpu.VMEM)
    hbm = pl.BlockSpec(memory_space=pltpu.HBM)
    dma = pltpu.SemaphoreType.DMA
    shapes = (jax.ShapeDtypeStruct(input_field.shape, BF16),
              jax.ShapeDtypeStruct(input_field.shape, BF16),
              jax.ShapeDtypeStruct((basis, blk, chans), BF16))
    results = pl.pallas_call(
        functools.partial(kernel_body, sizes),
        out_shape=shapes,
        in_specs=[hbm] * 5,
        out_specs=(hbm, hbm, hbm),
        scratch_shapes=[
            pltpu.VMEM((spans, rows + 2, basis, taps), BF16),
            pltpu.SMEM((nlat,), jnp.int32),
            pltpu.VMEM((rows, cols, chans), BF16),
            pltpu.VMEM((rows, cols, chans), BF16),
            pltpu.VMEM((basis, blk, chans), BF16),
            pltpu.VMEM((2, rows + 3, block, chans), BF16),
            pltpu.VMEM((2, rows + 2, side, chans), BF16),
            pltpu.VMEM((rows + 3, block, chans), BF16),
            pltpu.VMEM((2, rows + 2, side, chans), BF16),
            pltpu.VMEM((2, rows, cols, chans), BF16),
            pltpu.VMEM((basis, chans, chans), BF16),
            pltpu.VMEM((rows, basis * cols, lanes), BF16),
            pltpu.VMEM((rows, basis * cols, lanes), BF16),
            pltpu.VMEM((basis, 2 * rows, cols, chans), BF16),
            pltpu.VMEM((nq, 2, blk, 2 * rows * cols), BF16),
            pltpu.VMEM((ndp, nq, basis, blk, half), BF16),
            pltpu.VMEM((plane - 1, basis, blk, half), BF16),
            pltpu.VMEM((basis, blk, half), BF16),
            pltpu.VMEM((nz, blk, half), BF16),
            pltpu.VMEM((blk, half), BF16),
            dma((6,)), dma((19,)), dma((19,)), dma((groups, plane - 1)), dma((groups, plane - 1)),
            dma((basis,)), dma((nz,)), dma((nz * ndp,)), dma((basis * ndp,)),
            pltpu.SemaphoreType.REGULAR((4, 2)), pltpu.SemaphoreType.REGULAR((6,)),
            pltpu.SemaphoreType.REGULAR,
        ],
        compiler_params=pltpu.CompilerParams(
            collective_id=0, has_side_effects=True),
        name="disco_block",
    )(coeff, reach_cols, input_field, cotangent, channel_weight)
    anywhere = pl.BlockSpec(memory_space=pl.ANY)
    out, gin, gw = pl.pallas_call(
        hand_over,
        out_shape=shapes,
        in_specs=[vmem] * 3,
        out_specs=(hbm, hbm, hbm),
        scratch_shapes=[dma((3,))],
        name="hand_over",
    )(*results)
    return out, gin, jnp.transpose(gw, (0, 2, 1))


def solution(mesh):
    placed = (P("dp", "lat", "lon", None), P("dp", "lat", "lon", None), P(), P(), P())
    return jax.shard_map(
        on_device,
        mesh=mesh,
        in_specs=placed,
        out_specs=(P("dp", "lat", "lon", None), P("dp", "lat", "lon", None), P(None, None, "lon")),
        check_vma=False,
    )
```
